128 devices in a mesh: seq: 32 (over z, y, core), head: 4 (over x).
Axes of the slice: x: 4, y: 4, z: 4, core: 2. Of those that a mesh axis runs over, the one named last changes fastest.
Arguments:
- tokens: bfloat16 [8192, 4096], P('seq', 'head'), may hold values from -48 to 48
- queries: bfloat16 [8192, 4096], P('seq', 'head'), may hold values from -48 to 48
- valid_counts: int32 [32], P('seq'), may hold values from 64 to 256, as said below
- query_host: int32 [1], replicated, may hold values from 0 to 31
- w_query: bfloat16 [4096, 4096], P(None, 'head'), may hold values from -0.09375 to 0.09375
- w_key: bfloat16 [4096, 1024], P(None, 'head'), may hold values from -0.09375 to 0.09375
- w_value: bfloat16 [4096, 1024], P(None, 'head'), may hold values from -0.09375 to 0.09375
- w_out: bfloat16 [4096, 4096], P('head'), may hold values from -0.09375 to 0.09375
Outputs:
- block_out: bfloat16 [8192, 4096], P('seq', 'head')
- query_out: bfloat16 [256, 4096], P(None, 'head')
The draws below stay inside these ranges and needn't reach their ends.
Inputs may be any that keep to these rules, and one draw needn't show every extreme that they name: `valid_counts`: some block has all 256 tokens valid.
All inputs are finite; a program needn't handle non-finite values.
Results may differ from the reference program's by a relative error of at most 0.014.
The reference program's roundings to bfloat16 on the way count: a program that leaves them out, or rounds other values in their place, can miss the bound.
Values may be sent and summed in bfloat16 or wider, within the bound.
No kernel may reach another device: no remote copies, remote signals or barrier semaphores. Data moves between devices by JAX's collectives and lax.ppermute only.
A program may use at most 192 MiB of HBM per device.

```python
import jax
import jax.numpy as jnp
from jax import lax

D = 4096
HEADS = 32
KV_HEADS = 8
HD = 128
BLK = 256
QL = 256
CONTEXT = 8192
N_SEQ = 32


def rough_rows(key, count, width):
    first = jax.random.fold_in(key, 0)
    values = jax.random.normal(first, (count, width), jnp.float32)
    return jnp.clip(values, -6.0, 6.0)


def draw_tokens(key, part):
    key = jax.random.fold_in(key, 2)
    return rough_rows(key, CONTEXT, D).astype(jnp.bfloat16)


def draw_queries(key, part):
    key = jax.random.fold_in(key, 3)
    return rough_rows(key, QL * N_SEQ, D).astype(jnp.bfloat16)


def draw_valid_counts(key, part):
    key = jax.random.fold_in(key, 5)
    first, second = jax.random.split(key)
    counts = jax.random.randint(first, (N_SEQ,), BLK // 4, BLK + 1)
    chosen = jax.random.randint(second, (), 0, N_SEQ)
    return jnp.where(jnp.arange(N_SEQ) == chosen, BLK, counts).astype(jnp.int32)


def level_of(stream_key, shape, shards, least, largest):
    factor_of = 1.0
    for dim, blocks in shards:
        steps = jax.random.uniform(jax.random.fold_in(jax.random.fold_in(stream_key, 6), dim), (blocks,), jnp.float32, least / len(shards), largest / len(shards))
        factor_of = factor_of * jnp.repeat(jnp.exp(steps), shape[dim] // blocks).reshape((-1,) + (1,) * (len(shape) - 1 - dim))
    return factor_of


def scatter_about(own_key, shape, spread, limit, pieces=(), held_as=jnp.bfloat16):
    loudness = level_of(own_key, shape, pieces, -0.22, 0.18) if pieces else 1.0
    entries = jax.random.normal(own_key, shape, jnp.float32) * spread * loudness
    return jnp.minimum(jnp.maximum(entries, -limit), limit).astype(held_as)


def setup_inputs(seed: int = 0) -> dict:
    arg_keys = jax.random.split(jax.random.key(seed), 9)
    tokens = draw_tokens(jax.random.fold_in(arg_keys[8], 71), 0)
    queries = draw_queries(jax.random.fold_in(arg_keys[8], 71), 0)
    valid_counts = draw_valid_counts(jax.random.fold_in(arg_keys[8], 71), 0)
    query_host = jax.random.randint(arg_keys[3], (1,), 0, N_SEQ).astype(jnp.int32)
    w_query = scatter_about(arg_keys[4], (D, HEADS * HD), D ** -0.5, 0.09375, ((1, 4),))
    w_key = scatter_about(arg_keys[5], (D, KV_HEADS * HD), D ** -0.5, 0.09375, ((1, 4),))
    w_value = scatter_about(arg_keys[6], (D, KV_HEADS * HD), D ** -0.5, 0.09375, ((1, 4),))
    w_out = scatter_about(arg_keys[7], (HEADS * HD, D), (HEADS * HD) ** -0.5, 0.09375, ((0, 4),))
    return {"tokens": tokens, "queries": queries, "valid_counts": valid_counts, "query_host": query_host, "w_query": w_query, "w_key": w_key, "w_value": w_value, "w_out": w_out}


def project(rows, weight):
    return jnp.dot(rows, weight, preferred_element_type=jnp.float32).astype(jnp.bfloat16)


def scores_of(query, keys):
    count_q = query.shape[0]
    count_k = keys.shape[0]
    groups = keys.shape[1] // HD
    grouped = query.reshape(count_q, groups, -1, HD).astype(jnp.float32)
    keyed = keys.reshape(count_k, groups, HD).astype(jnp.float32)
    return jnp.einsum('rgqd,jgd->gqrj', grouped, keyed) * (HD ** -0.5)


def mix(weights, values):
    count_k = values.shape[0]
    groups = values.shape[1] // HD
    valued = values.reshape(count_k, groups, HD).astype(jnp.float32)
    return jnp.einsum('gqrj,jgd->gqrd', weights.astype(jnp.float32), valued)


def flatten(heads_out):
    return jnp.transpose(heads_out, (2, 0, 1, 3)).reshape(heads_out.shape[2], -1)


def partial_of(query, keys, values, visible):
    scores = jnp.where(visible, scores_of(query, keys), jnp.float32(-1e30))
    top = jnp.max(scores, axis=-1)
    weights = jnp.where(visible, jnp.exp(scores - top[..., None]), jnp.float32(0.0)).astype(jnp.bfloat16)
    total = jnp.sum(weights.astype(jnp.float32), axis=-1)
    return top, total, mix(weights, values)


def reference(tokens, queries, valid_counts, query_host, w_query, w_key, w_value, w_out):
    nblocks = valid_counts.shape[0]
    q_all = project(tokens, w_query)
    k_all = project(tokens, w_key)
    v_all = project(tokens, w_value)
    anchor_k = k_all[:BLK]
    anchor_v = v_all[:BLK]
    rows_i = jnp.arange(BLK)[:, None]
    cols_j = jnp.arange(BLK)[None, :]

    def one_block(index):
        start = (index * BLK).astype(jnp.int32)
        q_blk = lax.dynamic_slice_in_dim(q_all, start, BLK, 0)
        k_blk = lax.dynamic_slice_in_dim(k_all, start, BLK, 0)
        v_blk = lax.dynamic_slice_in_dim(v_all, start, BLK, 0)
        own = (cols_j <= rows_i) & (cols_j < valid_counts[index])
        front = jnp.broadcast_to((cols_j < valid_counts[0]) & (index > 0), (BLK, BLK))
        visible = jnp.concatenate([front, own], axis=1)
        keys = jnp.concatenate([anchor_k, k_blk], axis=0)
        values = jnp.concatenate([anchor_v, v_blk], axis=0)
        scores = jnp.where(visible, scores_of(q_blk, keys), jnp.float32(-1e30))
        weights = jax.nn.softmax(scores, axis=-1).astype(jnp.bfloat16)
        return flatten(mix(weights, values)).astype(jnp.bfloat16)

    ctx = lax.map(one_block, jnp.arange(nblocks, dtype=jnp.int32))
    ctx = ctx.reshape(nblocks * BLK, -1)
    block_out = jnp.dot(ctx, w_out, preferred_element_type=jnp.float32).astype(jnp.bfloat16)

    rows = lax.dynamic_slice_in_dim(queries, (query_host[0] * QL).astype(jnp.int32), QL, 0)
    q_q = project(rows, w_query)
    k_q = project(rows, w_key)
    v_q = project(rows, w_value)

    def one_partial(index):
        start = (index * BLK).astype(jnp.int32)
        k_blk = lax.dynamic_slice_in_dim(k_all, start, BLK, 0)
        v_blk = lax.dynamic_slice_in_dim(v_all, start, BLK, 0)
        visible = jnp.broadcast_to(jnp.arange(BLK)[None, :] < valid_counts[index], (QL, BLK))
        return partial_of(q_q, k_blk, v_blk, visible)

    tops, totals, outs = lax.map(one_partial, jnp.arange(nblocks, dtype=jnp.int32))
    causal = jnp.arange(QL)[None, :] <= jnp.arange(QL)[:, None]
    own_top, own_total, own_out = partial_of(q_q, k_q, v_q, causal)
    biggest = jnp.maximum(jnp.max(tops, axis=0), own_top)
    scale_b = jnp.exp(tops - biggest[None])
    scale_o = jnp.exp(own_top - biggest)
    denom = jnp.sum(totals * scale_b, axis=0) + own_total * scale_o
    numer = jnp.sum(outs * scale_b[..., None], axis=0) + own_out * scale_o[..., None]
    query_ctx = flatten(numer / denom[..., None]).astype(jnp.bfloat16)
    query_out = jnp.dot(query_ctx, w_out, preferred_element_type=jnp.float32).astype(jnp.bfloat16)
    return block_out, query_out
```

```python
import jax
import jax.numpy as jnp
from jax import lax
from jax.sharding import PartitionSpec as P

HD = 128
SCALE = HD ** (-0.5)
NEG = -1e30
PAIRS = 16
PLANE = [[2 * g + c for g in range(PAIRS)] for c in range(2)]
SWAP = [(i, i ^ 1) for i in range(2 * PAIRS)]


def project(rows, weight):
    return jnp.dot(rows, weight, preferred_element_type=jnp.float32).astype(jnp.bfloat16)


def scores_of(query, keys):
    groups = keys.shape[1] // HD
    grouped = query.reshape(query.shape[0], groups, -1, HD)
    keyed = keys.reshape(keys.shape[0], groups, HD)
    return (
        jnp.einsum("rgqd,jgd->gqrj", grouped, keyed, preferred_element_type=jnp.float32) * SCALE
    )


def mix(weights, values):
    valued = values.reshape(values.shape[0], -1, HD)
    return jnp.einsum("gqrj,jgd->rgqd", weights, valued, preferred_element_type=jnp.float32)


def plane_swap(blocks):
    return lax.all_to_all(blocks, "seq", 0, 0, axis_index_groups=PLANE, tiled=True)


def plane_gather(rows):
    copies = jnp.broadcast_to(rows[None], (PAIRS,) + rows.shape)
    return plane_swap(copies).reshape(PAIRS * rows.shape[0], rows.shape[1])


def core_swap(block):
    return lax.ppermute(block, "seq", SWAP)


def core_gather(block, core):
    other = core_swap(block)
    return jnp.where(
        core == 0,
        jnp.concatenate([block, other], axis=0),
        jnp.concatenate([other, block], axis=0),
    )


def half_of(array, which):
    half = array.shape[0] // 2
    return lax.dynamic_slice_in_dim(array, which * half, half, 0)


def local(tokens, queries, valid_counts, query_host, w_query, w_key, w_value, w_out):
    seq_index = lax.axis_index("seq")
    head_index = lax.axis_index("head")
    core = seq_index % 2
    pair = seq_index // 2
    host = query_host[0]
    local_count = valid_counts[0]
    blk = tokens.shape[0]
    width = tokens.shape[1]
    slab = blk // (2 * PAIRS)

    whole = lax.all_gather(tokens, "head", axis=1, tiled=True)

    rows_col = jnp.arange(blk)[:, None]
    marked = jnp.where(rows_col < local_count, tokens, jnp.bfloat16(jnp.nan))
    shared = jnp.stack([queries, marked], axis=1).reshape(2, PAIRS, slab, 2, width)
    shared = shared.transpose(0, 1, 3, 2, 4)
    keep = half_of(shared, core)[0]
    got = core_swap(half_of(shared, 1 - core)[0])
    from_got = jnp.stack([host % 2 != core, core != 0])[None, :, None, None]
    chosen = jnp.where(from_got, got, keep)
    spread = plane_swap(chosen)
    picked = jnp.concatenate(
        [lax.dynamic_index_in_dim(spread, host // 2, 0, False)[0], spread[0, 1]], axis=0
    )
    copies = jnp.broadcast_to(picked[None], (4,) + picked.shape)
    wide = lax.all_to_all(copies, "head", 0, 0, tiled=True)
    wide = wide.transpose(1, 0, 2).reshape(2 * slab, 4 * width)
    q_few = project(wide[:slab], w_query)
    k_few = project(wide, w_key)
    v_few = project(wide, w_value)
    packed = jnp.concatenate([q_few, k_few[slab:], v_few[slab:]], axis=1)
    everyone = core_gather(plane_gather(packed), core)
    q_wide = q_few.shape[1]
    kv_wide = k_few.shape[1]
    q_q = everyone[:, :q_wide]
    anchor_k = everyone[:, q_wide : q_wide + kv_wide]
    anchor_v = everyone[:, q_wide + kv_wide :]
    valid = anchor_k == anchor_k
    anchor_seen = valid[:, 0] & (seq_index > 0)
    anchor_k = jnp.where(valid, anchor_k, 0)
    anchor_v = jnp.where(anchor_v == anchor_v, anchor_v, 0)

    q_blk = project(whole, w_query)
    k_blk = project(whole, w_key)
    v_blk = project(whole, w_value)

    cols_j = jnp.arange(blk)[None, :]
    own = (cols_j <= rows_col) & (cols_j < local_count)
    front = jnp.broadcast_to(anchor_seen[None, :], (blk, blk))
    visible = jnp.concatenate([front, own], axis=1)
    keys = jnp.concatenate([anchor_k, k_blk], axis=0)
    values = jnp.concatenate([anchor_v, v_blk], axis=0)
    scores = jnp.where(visible, scores_of(q_blk, keys), jnp.float32(NEG))
    weights = jax.nn.softmax(scores, axis=-1).astype(jnp.bfloat16)
    block_ctx = mix(weights, values).reshape(blk, -1).astype(jnp.bfloat16)

    first_key = core * (blk // 2) + pair * slab
    itself = (first_key + jnp.arange(slab))[None, :] <= rows_col
    seen = jnp.concatenate([jnp.broadcast_to(cols_j < local_count, (blk, blk)), itself], axis=1)
    keys = jnp.concatenate([k_blk, k_few[:slab]], axis=0)
    values = jnp.concatenate([v_blk, v_few[:slab]], axis=0)
    scores = jnp.where(seen, scores_of(q_q, keys), jnp.float32(NEG))
    top = jnp.max(scores, axis=-1)
    weights = jnp.where(seen, jnp.exp(scores - top[..., None]), 0.0).astype(jnp.bfloat16)
    total = jnp.sum(weights.astype(jnp.float32), axis=-1)
    outs = mix(weights, values).reshape(blk, -1)
    heads = q_wide // HD
    top = top.reshape(heads, blk).T
    total = total.reshape(heads, blk).T
    pad = jnp.zeros((blk, HD - 2 * heads), jnp.float32)
    stats = jnp.concatenate([outs, top, total, pad], axis=1)

    def merge(parts):
        rows = parts.shape[1]
        o = parts[:, :, :q_wide].reshape(-1, rows, heads, HD)
        m = parts[:, :, q_wide : q_wide + heads]
        t = parts[:, :, q_wide + heads : q_wide + 2 * heads]
        biggest = jnp.max(m, axis=0)
        scale = jnp.exp(m - biggest[None])
        return biggest, jnp.sum(scale * t, axis=0), jnp.sum(scale[..., None] * o, axis=0)

    both = jnp.stack([half_of(stats, core), core_swap(half_of(stats, 1 - core))])
    m, t, o = merge(both)
    pad = jnp.zeros((blk // 2, HD - 2 * heads), jnp.float32)
    half = jnp.concatenate([o.reshape(blk // 2, -1), m, t, pad], axis=1)
    m, t, o = merge(plane_swap(half.reshape(PAIRS, slab, -1)))
    query_ctx = (o / t[..., None]).reshape(slab, -1).astype(jnp.bfloat16)
    query_term = jnp.dot(query_ctx, w_out, preferred_element_type=jnp.float32)
    query_term = query_term.reshape(slab, 4, width).transpose(1, 0, 2)
    query_sum = jnp.sum(lax.all_to_all(query_term, "head", 0, 0, tiled=True), axis=0)
    query_out = core_gather(plane_gather(query_sum.astype(jnp.bfloat16)), core)

    def term(step):
        columns = lax.dynamic_slice_in_dim(w_out, ((head_index + step) % 4) * width, width, 1)
        return jnp.dot(block_ctx, columns, preferred_element_type=jnp.float32)

    block_sum = term(0)
    for step in (2, 1, 3):
        partial = term(step).astype(jnp.bfloat16)
        block_sum += lax.ppermute(partial, "head", [(i, (i + step) % 4) for i in range(4)]).astype(
            jnp.float32
        )
    return (block_sum.astype(jnp.bfloat16), query_out)


def solution(mesh):
    return jax.shard_map(
        local,
        mesh=mesh,
        in_specs=(
            P("seq", "head"),
            P("seq", "head"),
            P("seq"),
            P(),
            P(None, "head"),
            P(None, "head"),
            P(None, "head"),
            P("head", None),
        ),
        out_specs=(P("seq", "head"), P(None, "head")),
        check_vma=False,
    )
```

```python
import jax
import jax.numpy as jnp
from jax import lax
from jax.experimental import pallas as pl
from jax.experimental.pallas import tpu as pltpu
from jax.sharding import PartitionSpec as P

HD = 128
SCALE = HD ** (-0.5)
NEG = -1e30
PAIRS = 16
PLANE = [[2 * g + c for g in range(PAIRS)] for c in range(2)]
SWAP = [(i, i ^ 1) for i in range(2 * PAIRS)]
MIB = 1 << 20


def params():
    return pltpu.CompilerParams(vmem_limit_bytes=56 * MIB, dimension_semantics=("arbitrary",))


def cost(flops, moved):
    return pl.CostEstimate(flops=flops, bytes_accessed=moved, transcendentals=0)


def plane_swap(blocks):
    return lax.all_to_all(blocks, "seq", 0, 0, axis_index_groups=PLANE, tiled=True)


def core_swap(block):
    return lax.ppermute(block, "seq", SWAP)


def head_shift(block, step):
    return lax.ppermute(block, "head", [(i, (i + step) % 4) for i in range(4)])


def exact_dot(a, b):
    return lax.dot_general(a, b, (((1,), (0,)), ((), ())), preferred_element_type=jnp.float32)


def score_dot(a, b):
    return lax.dot_general(a, b, (((1,), (1,)), ((), ())), preferred_element_type=jnp.float32)


def few_kernel(place, f0, f1, f2, f3, wq, wk, wv, pack_out, kv_out, acc):
    step = pl.program_id(0)
    steps = pl.num_programs(0)
    turn = (place[1] - step // (steps // 4) + 4) % 4
    few = jnp.where(
        turn == 0,
        f0[...],
        jnp.where(turn == 1, f1[...], jnp.where(turn == 2, f2[...], f3[...])),
    )
    nq, nk = wq.shape[1], wk.shape[1]

    @pl.when(step == 0)
    def _():
        acc[...] = jnp.zeros_like(acc)

    for ref, start, size in ((wq, 0, nq), (wk, nq, nk), (wv, nq + nk, nk)):
        acc[:, pl.ds(start, size)] += exact_dot(few, ref[...])

    @pl.when(step == steps - 1)
    def _():
        slab = few.shape[0] // 2
        pack = jnp.concatenate([acc[:slab, :nq], acc[slab:, nq:]], axis=1)
        pack_out[...] = jnp.broadcast_to(pack[None], pack_out.shape).astype(pack_out.dtype)
        own = jnp.concatenate([acc[:slab, nq:], jnp.zeros_like(acc[slab:, nq:])], axis=0)
        kv_out[...] = own.astype(kv_out.dtype)


def project_few(place, fews, w_query, w_key, w_value):
    steps = 8
    depth = w_query.shape[0]
    few = fews[0].shape[0]
    nq, nk = w_query.shape[1], w_key.shape[1]
    k = depth // steps
    per = steps // 4
    pack = (PAIRS, few // 2, nq + 2 * nk)
    return pl.pallas_call(
        few_kernel,
        grid_spec=pltpu.PrefetchScalarGridSpec(
            num_scalar_prefetch=1,
            grid=(steps,),
            in_specs=[pl.BlockSpec((few, k), lambda i, place: (0, i % per))] * 4
            + [
                pl.BlockSpec((k, nq), lambda i, place: (i, 0)),
                pl.BlockSpec((k, nk), lambda i, place: (i, 0)),
                pl.BlockSpec((k, nk), lambda i, place: (i, 0)),
            ],
            out_specs=[
                pl.BlockSpec(pack, lambda i, place: (0, 0, 0)),
                pl.BlockSpec((few, 2 * nk), lambda i, place: (0, 0)),
            ],
            scratch_shapes=[pltpu.VMEM((few, nq + 2 * nk), jnp.float32)],
        ),
        out_shape=[
            jax.ShapeDtypeStruct(pack, w_query.dtype),
            jax.ShapeDtypeStruct((few, 2 * nk), w_query.dtype),
        ],
        compiler_params=params(),
        cost_estimate=cost(2 * 128 * depth * (nq + 2 * nk), depth * (nq + 2 * nk) * 2),
    )(place, *fews, w_query, w_key, w_value)


def keys_kernel(rows, wk, wv, few, out, acc):
    step = pl.program_id(0)
    nk = wk.shape[1]
    count = rows.shape[0]
    for ref, start in ((wk, 0), (wv, nk)):
        part = exact_dot(rows[...], ref[...])
        here = pl.ds(start, nk)

        @pl.when(step == 0)
        def _():
            acc[:, here] = part

        @pl.when(step > 0)
        def _():
            acc[:, here] += part

    @pl.when(step == pl.num_programs(0) - 1)
    def _():
        out[:count, :] = acc[...].astype(out.dtype)
        out[count:, :] = few[...]


def project_keys(whole, w_key, w_value, few):
    steps = 4
    rows, depth = whole.shape
    nk = w_key.shape[1]
    k = depth // steps
    shape = (rows + few.shape[0], 2 * nk)
    return pl.pallas_call(
        keys_kernel,
        grid=(steps,),
        in_specs=[
            pl.BlockSpec((rows, k), lambda i: (0, i)),
            pl.BlockSpec((k, nk), lambda i: (i, 0)),
            pl.BlockSpec((k, nk), lambda i: (i, 0)),
            pl.BlockSpec(few.shape, lambda i: (0, 0)),
        ],
        out_specs=pl.BlockSpec(shape, lambda i: (0, 0)),
        out_shape=jax.ShapeDtypeStruct(shape, whole.dtype),
        scratch_shapes=[pltpu.VMEM((rows, 2 * nk), jnp.float32)],
        compiler_params=params(),
        cost_estimate=cost(2 * rows * depth * 2 * nk, 6 * MIB),
    )(whole, w_key, w_value, few)


def queries_kernel(rows, wq, out):
    out[...] = exact_dot(rows[...], wq[...]).astype(out.dtype)


def project_queries(whole, w_query):
    rows, depth = whole.shape
    wide = w_query.shape[1]
    n = wide // 4
    return pl.pallas_call(
        queries_kernel,
        grid=(4,),
        in_specs=[
            pl.BlockSpec((rows, depth), lambda i: (0, 0)),
            pl.BlockSpec((depth, n), lambda i: (0, i)),
        ],
        out_specs=pl.BlockSpec((rows, n), lambda i: (0, i)),
        out_shape=jax.ShapeDtypeStruct((rows, wide), whole.dtype),
        compiler_params=params(),
        cost_estimate=cost(2 * rows * depth * wide, 10 * MIB),
    )(whole, w_query)


def query_kernel(place, counts, sibling, q_ref, mine, other, out):
    core, pair, count_mine, count_other = place[0], place[2], counts[0], sibling[0]
    half = q_ref.shape[0] * q_ref.shape[1]
    blk = 2 * half
    nk = mine.shape[1] // 2
    few = mine.shape[0] - blk
    slab = few // 2
    groups = nk // HD
    heads = q_ref.shape[2] // HD
    q = q_ref[...].reshape(half, q_ref.shape[2])
    local_row = lax.broadcasted_iota(jnp.int32, (half, HD), 0)
    row = local_row + slab * (local_row // slab + core)
    lane = lax.broadcasted_iota(jnp.int32, (half, HD), 1)
    col = lax.broadcasted_iota(jnp.int32, (half, blk), 1)
    first = (2 * pair + core) * slab
    first_other = (2 * pair + 1 - core) * slab
    own_a = (lane < slab) & (first + lane <= row)
    own_b = (lane >= few) & (lane < few + slab) & (first_other + lane - few <= row)
    seen = jnp.concatenate([col < count_mine, col < count_other, own_a | own_b], axis=1)
    fill = jnp.zeros((HD - 2 * few, HD), mine.dtype)
    stats = jnp.zeros((half, HD), jnp.float32)
    for g in range(groups):
        kc, vc = pl.ds(g * HD, HD), pl.ds(nk + g * HD, HD)
        keys, values = (
            jnp.concatenate(
                [mine[:blk, c], other[:blk, c], mine[blk:, c], other[blk:, c], fill], axis=0
            )
            for c in (kc, vc)
        )
        for h in range(g * (heads // groups), (g + 1) * (heads // groups)):
            s = score_dot(q[:, h * HD : (h + 1) * HD], keys) * SCALE
            s = jnp.where(seen, s, NEG)
            top = jnp.max(s, axis=1, keepdims=True)
            p = jnp.where(seen, jnp.exp(s - top), 0.0).astype(mine.dtype)
            total = jnp.sum(p.astype(jnp.float32), axis=1, keepdims=True)
            o = exact_dot(p, values)
            out[:, :, pl.ds(h * HD, HD)] = o.reshape(out.shape[0], out.shape[1], HD)
            stats = jnp.where(lane == h, top, jnp.where(lane == heads + h, total, stats))
    out[:, :, pl.ds(heads * HD, HD)] = stats.reshape(out.shape[0], out.shape[1], HD)


def query_attention(place, counts, sibling, mine_rows, kv, kv_other):
    pairs, slab, wide = mine_rows.shape
    nq = wide - kv.shape[1]
    shape = (pairs, slab, nq + HD)
    whole = lambda i, *_: (0, 0)
    return pl.pallas_call(
        query_kernel,
        grid_spec=pltpu.PrefetchScalarGridSpec(
            num_scalar_prefetch=3,
            grid=(1,),
            in_specs=[
                pl.BlockSpec((pairs, slab, nq), lambda i, *_: (0, 0, 0)),
                pl.BlockSpec(kv.shape, whole),
                pl.BlockSpec(kv.shape, whole),
            ],
            out_specs=pl.BlockSpec(shape, lambda i, *_: (0, 0, 0)),
        ),
        out_shape=jax.ShapeDtypeStruct(shape, jnp.float32),
        compiler_params=params(),
        cost_estimate=cost(4 * pairs * slab * 640 * nq, 4 * MIB),
    )(place, counts, sibling, mine_rows, kv, kv_other)


def context_kernel(place, counts, q_ref, kv, a_mine, a_other, w_ref, out, own, ctx):
    step = pl.program_id(0)
    core, seq, count = place[0], place[3], counts[0]
    blk = q_ref.shape[0]
    half = blk // 2
    nk = kv.shape[1] // 2
    groups = nk // HD
    heads = q_ref.shape[1] // HD

    @pl.when(step == 0)
    def _():
        anchor = jnp.concatenate([a_mine[...].reshape(half, 2 * nk), a_other[...]], axis=0)
        row = lax.broadcasted_iota(jnp.int32, (blk, blk), 0)
        col = lax.broadcasted_iota(jnp.int32, (blk, blk), 1)
        seen = (col <= row) & (col < count)
        front = jnp.zeros((blk, blk), jnp.int32) + seq > 0
        for g in range(groups):
            ka = anchor[:, g * HD : (g + 1) * HD]
            va = anchor[:, nk + g * HD : nk + (g + 1) * HD].astype(jnp.float32)
            va = jnp.where(va == va, va, 0.0).astype(kv.dtype)
            kb = kv[:blk, pl.ds(g * HD, HD)]
            vb = kv[:blk, pl.ds(nk + g * HD, HD)]
            values = jnp.concatenate([va, vb], axis=0)
            for h in range(g * (heads // groups), (g + 1) * (heads // groups)):
                q = q_ref[:, pl.ds(h * HD, HD)]
                sa = score_dot(q, ka) * SCALE
                sa = jnp.where(front & (sa == sa), sa, NEG)
                sb = jnp.where(seen, score_dot(q, kb) * SCALE, NEG)
                s = jnp.concatenate([sa, sb], axis=1)
                p = jnp.exp(s - jnp.max(s, axis=1, keepdims=True))
                p = p / jnp.sum(p, axis=1, keepdims=True)
                ctx[:, pl.ds(h * HD, HD)] = exact_dot(p.astype(kv.dtype), values).astype(ctx.dtype)

    part = exact_dot(ctx[...], w_ref[...])

    @pl.when(step < 3)
    def _():
        out[0] = part.astype(out.dtype)

    @pl.when(step == 3)
    def _():
        own[...] = part


def context(place, counts, q, kv, a_mine, a_other, w_out):
    blk, nq = q.shape
    depth, wide = w_out.shape
    width = wide // 4
    pairs, slab, full = a_mine.shape
    nkv = kv.shape[1]
    whole = lambda i, place, counts: (0, 0)
    order = lambda i, place, counts: (0, (place[1] + jnp.where(i == 0, 2, jnp.where(i == 1, 1, jnp.where(i == 2, 3, 0)))) % 4)
    return pl.pallas_call(
        context_kernel,
        grid_spec=pltpu.PrefetchScalarGridSpec(
            num_scalar_prefetch=2,
            grid=(4,),
            in_specs=[
                pl.BlockSpec(q.shape, whole),
                pl.BlockSpec(kv.shape, whole),
                pl.BlockSpec((pairs, slab, nkv), lambda i, place, counts: (0, 0, full // nkv - 1)),
                pl.BlockSpec(a_other.shape, whole),
                pl.BlockSpec((depth, width), order),
            ],
            out_specs=[
                pl.BlockSpec((1, blk, width), lambda i, place, counts: (jnp.minimum(i, 2), 0, 0)),
                pl.BlockSpec((blk, width), whole),
            ],
            scratch_shapes=[pltpu.VMEM((blk, nq), q.dtype)],
        ),
        out_shape=[
            jax.ShapeDtypeStruct((3, blk, width), q.dtype),
            jax.ShapeDtypeStruct((blk, width), jnp.float32),
        ],
        compiler_params=params(),
        cost_estimate=cost(4 * blk * 512 * nq + 2 * blk * depth * wide, 12 * MIB),
    )(place, counts, q, kv, a_mine, a_other, w_out)


def merge_kernel(place, parts, w_ref, out, ctx):
    step = pl.program_id(0)
    heads = (parts.shape[2] - HD) // HD

    @pl.when(step == 0)
    def _():
        m = parts[:, :, pl.ds(heads * HD, heads)]
        t = parts[:, :, pl.ds(heads * HD + heads, heads)]
        scale = jnp.exp(m - jnp.max(m, axis=0, keepdims=True))
        total = jnp.sum(scale * t, axis=0)
        for h in range(heads):
            o = parts[:, :, pl.ds(h * HD, HD)]
            o = jnp.sum(scale[:, :, h : h + 1] * o, axis=0) / total[:, h : h + 1]
            ctx[:, pl.ds(h * HD, HD)] = o.astype(ctx.dtype)

    out[0] = exact_dot(ctx[...], w_ref[...])


def merge(place, parts, w_out):
    pairs, slab, full = parts.shape
    depth, wide = w_out.shape
    width = wide // 4
    return pl.pallas_call(
        merge_kernel,
        grid_spec=pltpu.PrefetchScalarGridSpec(
            num_scalar_prefetch=1,
            grid=(4,),
            in_specs=[
                pl.BlockSpec(parts.shape, lambda i, place: (0, 0, 0)),
                pl.BlockSpec((depth, width), lambda i, place: (0, (place[1] + i) % 4)),
            ],
            out_specs=pl.BlockSpec((1, slab, width), lambda i, place: (i, 0, 0)),
            scratch_shapes=[pltpu.VMEM((slab, depth), w_out.dtype)],
        ),
        out_shape=jax.ShapeDtypeStruct((4, slab, width), jnp.float32),
        compiler_params=params(),
        cost_estimate=cost(2 * 128 * depth * wide, depth * wide * 2),
    )(place, parts, w_out)


def total_kernel(a, b, c, d, out):
    total = (a[0] + b[0]) + (c[0] + d[0])
    out[...] = jnp.broadcast_to(total[None], out.shape).astype(out.dtype)


def local(tokens, queries, valid_counts, query_host, w_query, w_key, w_value, w_out):
    seq_index = lax.axis_index("seq").astype(jnp.int32)
    head_index = lax.axis_index("head").astype(jnp.int32)
    core = seq_index % 2
    pair = seq_index // 2
    host = query_host[0]
    blk, width = tokens.shape
    slab = blk // (2 * PAIRS)
    dtype = tokens.dtype
    nq = w_query.shape[1]
    place = jnp.stack([core, head_index, pair, seq_index])

    whole = lax.all_gather(tokens, "head", axis=1, tiled=True)
    sibling = core_swap(valid_counts)
    got = core_swap(tokens)

    count = jnp.where(core == 0, valid_counts[0], sibling[0])
    anchor = jnp.where(core == 0, tokens, got)
    anchor = jnp.where(jnp.arange(blk)[:, None] < count, anchor, jnp.bfloat16(jnp.nan))
    sent = jnp.where(seq_index == host, queries, anchor)
    spread = lax.all_to_all(sent, "seq", 0, 0, tiled=True)
    source = jnp.where(host == 1, 0, 1)
    picked = jnp.concatenate(
        [lax.dynamic_slice_in_dim(spread, at * slab, slab, 0) for at in (host, source)], axis=0
    )
    fews = [picked] + [head_shift(picked, step) for step in (1, 2, 3)]
    pack, few_kv = project_few(place, fews, w_query, w_key, w_value)
    mine = plane_swap(pack)
    whole, few_kv = lax.optimization_barrier((whole, few_kv))
    kv = project_keys(whole, w_key, w_value, few_kv)
    kv_other = core_swap(kv)
    q_blk = project_queries(whole, w_query)
    anchor_other = core_swap(mine[:, :, nq:].reshape(blk // 2, -1))

    stats = query_attention(place, valid_counts, sibling, mine, kv, kv_other)
    merged = plane_swap(stats)
    partial, own = context(place, valid_counts, q_blk, kv, mine, anchor_other, w_out)
    near = [head_shift(partial[at], step) for at, step in ((1, 1), (2, 3))]
    term = merge(place, merged, w_out)
    parts = [term[:1]] + [head_shift(term[step : step + 1], step) for step in (1, 2, 3)]
    copies = pl.pallas_call(
        total_kernel,
        out_shape=jax.ShapeDtypeStruct((2 * PAIRS, slab, width), dtype),
    )(*parts)
    far, copies = lax.optimization_barrier((partial[0], copies))
    far = head_shift(far, 2)
    query_out = lax.all_to_all(copies, "seq", 0, 0, tiled=True).reshape(blk, width)
    block_sum = own
    for part in near + [far]:
        block_sum += part.astype(jnp.float32)
    return (block_sum.astype(dtype), query_out)


def solution(mesh):
    return jax.shard_map(
        local,
        mesh=mesh,
        in_specs=(
            P("seq", "head"),
            P("seq", "head"),
            P("seq"),
            P(),
            P(None, "head"),
            P(None, "head"),
            P(None, "head"),
            P("head", None),
        ),
        out_specs=(P("seq", "head"), P(None, "head")),
        check_vma=False,
    )
```

```python
import jax
import jax.numpy as jnp
from jax import lax
from jax.experimental import pallas as pl
from jax.experimental.pallas import tpu as pltpu
from jax.sharding import PartitionSpec as P

HD = 128
LOG2_SCALE = HD ** (-0.5) * 1.4426950408889634
NEG = -1e30
PAIRS = 16
PLANE = [[2 * g + c for g in range(PAIRS)] for c in range(2)]
SWAP = [(i, i ^ 1) for i in range(2 * PAIRS)]
MIB = 1 << 20


def params(mib=56):
    return pltpu.CompilerParams(vmem_limit_bytes=mib * MIB)


def cost(flops, moved):
    return pl.CostEstimate(flops=flops, bytes_accessed=moved, transcendentals=0)


def plane_swap(blocks):
    return lax.all_to_all(blocks, "seq", 0, 0, axis_index_groups=PLANE, tiled=True)


def core_swap(block):
    return lax.ppermute(block, "seq", SWAP)


def head_shift(block, step):
    return lax.ppermute(block, "head", [(i, (i + step) % 4) for i in range(4)])


def exact_dot(a, b):
    return lax.dot_general(a, b, (((1,), (0,)), ((), ())), preferred_element_type=jnp.float32)


def score_dot(a, b):
    return lax.dot_general(a, b, (((1,), (1,)), ((), ())), preferred_element_type=jnp.float32)


def start_all(copies):
    for copy in copies:
        copy.start()
    return copies


def rows_of(place, step, size):
    return pl.ds(pl.multiple_of(((place[1] - step + 4) % 4) * size, size), size)


def few_kernel(place, f0, f1, f2, f3, wq, wk, wv, pack_out, kv_out, held_q, held_kv, sems):
    fews = (f0, f1, f2, f3)
    size = f0.shape[1]
    nk = wk.shape[1]
    copies = []
    for step in range(4):
        rows = rows_of(place, step, size)
        copies.append(
            start_all(
                [
                    pltpu.make_async_copy(wq.at[rows], held_q.at[step], sems.at[step, 0]),
                    pltpu.make_async_copy(wk.at[rows], held_kv.at[step, 0], sems.at[step, 1]),
                    pltpu.make_async_copy(wv.at[rows], held_kv.at[step, 1], sems.at[step, 2]),
                ]
            )
        )
    q = k = v = 0.0
    for step in range(4):
        for copy in copies[step]:
            copy.wait()
        few = fews[step][...]
        q += exact_dot(few, held_q[step])
        k += exact_dot(few, held_kv[step, 0])
        v += exact_dot(few, held_kv[step, 1])
    slab = f0.shape[0] // 2
    pack = jnp.concatenate([q[:slab], k[slab:], v[slab:]], axis=1)
    pack_out[...] = jnp.broadcast_to(pack[None], pack_out.shape).astype(pack_out.dtype)
    own = jnp.concatenate([k[:slab], v[:slab]], axis=1)
    kv_out[...] = jnp.concatenate([own, jnp.zeros_like(own)], axis=0).astype(kv_out.dtype)


VMEM = pl.BlockSpec(memory_space=pltpu.VMEM)
SMEM = pl.BlockSpec(memory_space=pltpu.SMEM)
ANY = pl.BlockSpec(memory_space=pl.ANY)
HBM = pl.BlockSpec(memory_space=pltpu.HBM)


def project_few(place, fews, w_query, w_key, w_value):
    depth = w_query.shape[0]
    few, size = fews[0].shape
    nq, nk = w_query.shape[1], w_key.shape[1]
    dtype = w_query.dtype
    return pl.pallas_call(
        few_kernel,
        in_specs=[SMEM] + [VMEM] * 4 + [HBM] * 3,
        out_specs=[VMEM] * 2,
        out_shape=[
            jax.ShapeDtypeStruct((PAIRS, few // 2, nq + 2 * nk), dtype),
            jax.ShapeDtypeStruct((few, 2 * nk), dtype),
        ],
        scratch_shapes=[
            pltpu.VMEM((4, size, nq), dtype),
            pltpu.VMEM((4, 2, size, nk), dtype),
            pltpu.SemaphoreType.DMA((4, 3)),
        ],
        compiler_params=params(),
        cost_estimate=cost(2 * 128 * depth * (nq + 2 * nk), depth * (nq + 2 * nk) * 2),
    )(place, *fews, w_query, w_key, w_value)


def chunk_copies(chunk, held, sems, at):
    if not isinstance(chunk, tuple):
        return [pltpu.make_async_copy(chunk, held, sems.at[at])]
    half = chunk[0].shape[0]
    return [
        pltpu.make_async_copy(part, held.at[pl.ds(i * half, half)], sems.at[at + i])
        for i, part in enumerate(chunk)
    ]


def keys_kernel(place, c0, c1, c2a, c2b, c3, wk, wv, few, out, held, held_kv, acc, sems):
    chunks = (c0, c1, (c2a, c2b), c3)
    count, size = c0.shape
    nk = wk.shape[1]
    copies = []
    for step in range(4):
        rows = rows_of(place, step, size)
        copies.append(
            start_all(
                [
                    pltpu.make_async_copy(wk.at[rows], held_kv.at[step, 0], sems.at[step, 0]),
                    pltpu.make_async_copy(wv.at[rows], held_kv.at[step, 1], sems.at[step, 1]),
                ]
                + chunk_copies(chunks[step], held.at[step], sems.at[step], 2)
            )
        )
    for step in range(4):
        for copy in copies[step]:
            copy.wait()
        for part in range(2):
            here = pl.ds(part * nk, nk)
            term = exact_dot(held[step], held_kv[step, part])
            if step == 0:
                acc[:, here] = term
            elif step < 3:
                acc[:, here] += term
            else:
                out[:count, here] = (acc[:, here] + term).astype(out.dtype)
    out[count:, :] = few[...]


def project_keys(place, chunks, w_key, w_value, few):
    rows, size = chunks[0].shape
    nk = w_key.shape[1]
    shape = (rows + few.shape[0], 2 * nk)
    dtype = w_key.dtype
    return pl.pallas_call(
        keys_kernel,
        in_specs=[SMEM] + [ANY] * 5 + [HBM] * 2 + [VMEM],
        out_specs=VMEM,
        out_shape=jax.ShapeDtypeStruct(shape, dtype),
        scratch_shapes=[
            pltpu.VMEM((4, rows, size), dtype),
            pltpu.VMEM((4, 2, size, nk), dtype),
            pltpu.VMEM((rows, 2 * nk), jnp.float32),
            pltpu.SemaphoreType.DMA((4, 4)),
        ],
        compiler_params=params(),
        cost_estimate=cost(2 * rows * 4 * size * 2 * nk, 6 * MIB),
    )(place, *chunks, w_key, w_value, few)


def queries_kernel(place, c0, c1, c2a, c2b, c3, wq, out, held, held_q, acc, sems):
    chunks = (c0, c1, (c2a, c2b), c3)
    count, size = c0.shape
    copies = []
    for step in range(4):
        rows = rows_of(place, step, size)
        copies.append(
            start_all(
                [
                    pltpu.make_async_copy(wq.at[rows], held_q.at[step], sems.at[step, 0]),
                ]
                + chunk_copies(chunks[step], held.at[step], sems.at[step], 1)
            )
        )
    for step in range(4):
        for copy in copies[step]:
            copy.wait()
        term = exact_dot(held[step], held_q[step])
        if step == 0:
            acc[...] = term
        elif step < 3:
            acc[...] += term
        else:
            out[...] = (acc[...] + term).astype(out.dtype)


def project_queries(place, chunks, w_query):
    rows, size = chunks[0].shape
    wide = w_query.shape[1]
    dtype = w_query.dtype
    return pl.pallas_call(
        queries_kernel,
        in_specs=[SMEM] + [ANY] * 5 + [HBM],
        out_specs=VMEM,
        out_shape=jax.ShapeDtypeStruct((rows, wide), dtype),
        scratch_shapes=[
            pltpu.VMEM((4, rows, size), dtype),
            pltpu.VMEM((4, size, wide), dtype),
            pltpu.VMEM((rows, wide), jnp.float32),
            pltpu.SemaphoreType.DMA((4, 3)),
        ],
        compiler_params=params(),
        cost_estimate=cost(2 * rows * 4 * size * wide, 10 * MIB),
    )(place, *chunks, w_query)


def query_kernel(place, counts, sibling, q_ref, mine, other, out):
    core, pair, count_mine, count_other = place[0], place[2], counts[0], sibling[0]
    half = q_ref.shape[0] * q_ref.shape[1]
    blk = 2 * half
    nk = mine.shape[1] // 2
    few = mine.shape[0] - blk
    slab = few // 2
    groups = nk // HD
    wide = q_ref.shape[2] - 2 * nk
    heads = wide // HD
    q = q_ref[:, :, :wide].reshape(half, wide)
    local_row = lax.broadcasted_iota(jnp.int32, (half, HD), 0)
    row = local_row + slab * (local_row // slab + core)
    lane = lax.broadcasted_iota(jnp.int32, (half, HD), 1)
    col = lax.broadcasted_iota(jnp.int32, (half, blk), 1)
    first = (2 * pair + core) * slab
    first_other = (2 * pair + 1 - core) * slab
    own_a = (lane < slab) & (first + lane <= row)
    own_b = (lane >= few) & (lane < few + slab) & (first_other + lane - few <= row)
    seen = jnp.concatenate([col < count_mine, col < count_other, own_a | own_b], axis=1)
    fill = jnp.zeros((HD - 2 * few, HD), mine.dtype)
    stats = jnp.zeros((half, HD), jnp.float32)
    for g in range(groups):
        kc, vc = pl.ds(g * HD, HD), pl.ds(nk + g * HD, HD)
        keys, values = (
            jnp.concatenate(
                [mine[:blk, c], other[:blk, c], mine[blk:, c], other[blk:, c], fill], axis=0
            )
            for c in (kc, vc)
        )
        for h in range(g * (heads // groups), (g + 1) * (heads // groups)):
            s = jnp.where(seen, score_dot(q[:, h * HD : (h + 1) * HD], keys), NEG)
            top = jnp.max(s, axis=1, keepdims=True)
            p = jnp.exp2((s - top) * LOG2_SCALE).astype(mine.dtype)
            total = jnp.sum(p.astype(jnp.float32), axis=1, keepdims=True)
            o = exact_dot(p, values)
            out[:, :, pl.ds(h * HD, HD)] = o.reshape(out.shape[0], out.shape[1], HD)
            stats = jnp.where(lane == h, top, jnp.where(lane == heads + h, total, stats))
    out[:, :, pl.ds(heads * HD, HD)] = stats.reshape(out.shape[0], out.shape[1], HD)


def query_attention(place, counts, sibling, mine_rows, kv, kv_other):
    pairs, slab, wide = mine_rows.shape
    nq = wide - kv.shape[1]
    return pl.pallas_call(
        query_kernel,
        in_specs=[SMEM] * 3 + [VMEM] * 3,
        out_specs=VMEM,
        out_shape=jax.ShapeDtypeStruct((pairs, slab, nq + HD), jnp.float32),
        compiler_params=params(24),
        cost_estimate=cost(4 * pairs * slab * 640 * nq, 4 * MIB),
    )(place, counts, sibling, mine_rows, kv, kv_other)


ORDER = (2, 1, 3, 0)


def columns_of(place, step, size):
    return pl.ds(pl.multiple_of(((place[1] + step) % 4) * size, size), size)


def context_kernel(
    place, counts, q_ref, kv, a_mine, a_other, w_ref, out0, out1, out2, own, ctx, held, sems
):
    seq, count = place[3], counts[0]
    blk = q_ref.shape[0]
    width = own.shape[1]
    half = blk // 2
    nk = kv.shape[1] // 2
    groups = nk // HD
    heads = q_ref.shape[1] // HD
    copies = [
        pltpu.make_async_copy(w_ref.at[:, columns_of(place, turn, width)], held.at[at], sems.at[at])
        for at, turn in enumerate(ORDER)
    ]
    start_all(copies)
    row = lax.broadcasted_iota(jnp.int32, (blk, blk), 0)
    col = lax.broadcasted_iota(jnp.int32, (blk, blk), 1)
    own_seen = (col <= row) & (col < count)
    front = jnp.zeros((blk, blk), jnp.int32) + seq > 0
    nq = q_ref.shape[1]
    for g in range(groups):
        kc, vc = pl.ds(g * HD, HD), pl.ds(nk + g * HD, HD)
        ac, bc = pl.ds(nq + g * HD, HD), pl.ds(nq + nk + g * HD, HD)
        ka = jnp.concatenate([r[:, :, ac].reshape(half, HD) for r in (a_mine, a_other)], axis=0)
        va = jnp.concatenate([r[:, :, bc].reshape(half, HD) for r in (a_mine, a_other)], axis=0)
        va = va.astype(jnp.float32)
        va = jnp.where(va == va, va, 0.0).astype(kv.dtype)
        keys = jnp.concatenate([ka, kv[:blk, kc]], axis=0)
        values = jnp.concatenate([va, kv[:blk, vc]], axis=0)
        seen = None
        for h in range(g * (heads // groups), (g + 1) * (heads // groups)):
            s = score_dot(q_ref[:, pl.ds(h * HD, HD)], keys)
            if seen is None:
                seen = jnp.concatenate([front & (s[:, :blk] == s[:, :blk]), own_seen], axis=1)
            s = jnp.where(seen, s, NEG)
            p = jnp.exp2((s - jnp.max(s, axis=1, keepdims=True)) * LOG2_SCALE)
            p = p * (1.0 / jnp.sum(p, axis=1, keepdims=True))
            ctx[:, pl.ds(h * HD, HD)] = exact_dot(p.astype(kv.dtype), values).astype(ctx.dtype)
    for at in range(4):
        copies[at].wait()
        part = exact_dot(ctx[...], held[at])
        (out0, out1, out2, own)[at][...] = part.astype((out0, own)[at // 3].dtype)


def context(place, counts, q, kv, a_mine, a_other, w_out):
    blk, nq = q.shape
    depth, wide = w_out.shape
    width = wide // 4
    return pl.pallas_call(
        context_kernel,
        in_specs=[SMEM] * 2 + [VMEM] * 4 + [HBM],
        out_specs=[VMEM] * 4,
        out_shape=[jax.ShapeDtypeStruct((blk, width), q.dtype)] * 3
        + [jax.ShapeDtypeStruct((blk, width), jnp.float32)],
        scratch_shapes=[
            pltpu.VMEM((blk, nq), q.dtype),
            pltpu.VMEM((4, depth, width), q.dtype),
            pltpu.SemaphoreType.DMA((4,)),
        ],
        compiler_params=params(),
        cost_estimate=cost(4 * blk * 512 * nq + 2 * blk * depth * wide, 12 * MIB),
    )(place, counts, q, kv, a_mine, a_other, w_out)


def merge_kernel(place, parts, w_ref, out0, out1, out2, out3, held, sems):
    width = out0.shape[1]
    heads = (parts.shape[2] - HD) // HD
    copies = [
        pltpu.make_async_copy(w_ref.at[:, columns_of(place, at, width)], held.at[at], sems.at[at])
        for at in range(4)
    ]
    start_all(copies)
    m = parts[:, :, pl.ds(heads * HD, heads)]
    t = parts[:, :, pl.ds(heads * HD + heads, heads)]
    scale = jnp.exp2((m - jnp.max(m, axis=0, keepdims=True)) * LOG2_SCALE)
    total = jnp.sum(scale * t, axis=0)
    ctx = []
    for h in range(heads):
        o = parts[:, :, pl.ds(h * HD, HD)]
        ctx.append(jnp.sum(scale[:, :, h : h + 1] * o, axis=0) / total[:, h : h + 1])
    ctx = jnp.concatenate(ctx, axis=1).astype(w_ref.dtype)
    for at in range(4):
        copies[at].wait()
        (out0, out1, out2, out3)[at][...] = exact_dot(ctx, held[at])


def merge(place, parts, w_out):
    slab = parts.shape[1]
    depth, wide = w_out.shape
    width = wide // 4
    return pl.pallas_call(
        merge_kernel,
        in_specs=[SMEM, VMEM, HBM],
        out_specs=[VMEM] * 4,
        out_shape=[jax.ShapeDtypeStruct((slab, width), jnp.float32)] * 4,
        scratch_shapes=[
            pltpu.VMEM((4, depth, width), w_out.dtype),
            pltpu.SemaphoreType.DMA((4,)),
        ],
        compiler_params=params(),
        cost_estimate=cost(2 * 128 * depth * wide, depth * wide * 2),
    )(place, parts, w_out)


def total_kernel(a, b, c, d, out):
    total = (a[...] + b[...]) + (c[...] + d[...])
    out[...] = jnp.broadcast_to(total[None], out.shape).astype(out.dtype)


def local(tokens, queries, valid_counts, query_host, w_query, w_key, w_value, w_out):
    seq_index = lax.axis_index("seq").astype(jnp.int32)
    head_index = lax.axis_index("head").astype(jnp.int32)
    core = seq_index % 2
    pair = seq_index // 2
    host = query_host[0]
    blk, width = tokens.shape
    slab = blk // (2 * PAIRS)
    dtype = tokens.dtype
    place = jnp.stack([core, head_index, pair, seq_index])

    right, left = head_shift(tokens, 1), head_shift(tokens, 3)
    sibling = core_swap(valid_counts)
    got = core_swap(tokens)

    count = jnp.where(core == 0, valid_counts[0], sibling[0])
    anchor = jnp.where(core == 0, tokens, got)
    anchor = jnp.where(jnp.arange(blk)[:, None] < count, anchor, jnp.bfloat16(jnp.nan))
    sent = jnp.where(seq_index == host, queries, anchor)
    spread = lax.all_to_all(sent, "seq", 0, 0, tiled=True)
    source = jnp.where(host == 1, 0, 1)
    picked = jnp.concatenate(
        [lax.dynamic_slice_in_dim(spread, at * slab, slab, 0) for at in (host, source)], axis=0
    )
    fews = [picked] + [head_shift(picked, step) for step in (1, 2, 3)]
    right_half, left_half, *fews = lax.optimization_barrier((right[: blk // 2], left[blk // 2 :], *fews))
    chunks = [tokens, right, head_shift(right_half, 1), head_shift(left_half, 3), left]
    pack, few_kv = project_few(place, fews, w_query, w_key, w_value)
    mine = plane_swap(pack)
    kv = project_keys(place, chunks, w_key, w_value, few_kv)
    kv_other = core_swap(kv)
    q_blk = project_queries(place, chunks, w_query)
    mine, q_blk = lax.optimization_barrier((mine, q_blk))
    mine_other = core_swap(mine)

    stats = query_attention(place, valid_counts, sibling, mine, kv, kv_other)
    merged = plane_swap(stats)
    *partial, own = context(place, valid_counts, q_blk, kv, mine, mine_other, w_out)
    merged, own, *partial = lax.optimization_barrier((merged, own, *partial))
    term = merge(place, merged, w_out)
    parts = [term[0]] + [head_shift(term[step], step) for step in (1, 2, 3)]
    *near, _ = lax.optimization_barrier((partial[1], partial[2], term[0]))
    near = [head_shift(near[at], step) for at, step in ((0, 1), (1, 3))]
    copies = pl.pallas_call(
        total_kernel,
        out_shape=jax.ShapeDtypeStruct((2 * PAIRS, slab, width), dtype),
        compiler_params=params(24),
    )(*parts)
    far, copies = lax.optimization_barrier((partial[0], copies))
    far = head_shift(far, 2)
    query_out = lax.all_to_all(copies, "seq", 0, 0, tiled=True).reshape(blk, width)
    block_sum = own
    for part in near + [far]:
        block_sum += part.astype(jnp.float32)
    return (block_sum.astype(dtype), query_out)


def solution(mesh):
    return jax.shard_map(
        local,
        mesh=mesh,
        in_specs=(
            P("seq", "head"),
            P("seq", "head"),
            P("seq"),
            P(),
            P(None, "head"),
            P(None, "head"),
            P(None, "head"),
            P("head", None),
        ),
        out_specs=(P("seq", "head"), P(None, "head")),
        check_vma=False,
    )
```

```python
import jax
import jax.numpy as jnp
from jax import lax
from jax.experimental import pallas as pl
from jax.experimental.pallas import tpu as pltpu
from jax.sharding import PartitionSpec as P

HD = 128
LOG2_SCALE = HD ** (-0.5) * 1.4426950408889634
NEG = -1e30
PAIRS = 16
PLANE = [[2 * g + c for g in range(PAIRS)] for c in range(2)]
SWAP = [(i, i ^ 1) for i in range(2 * PAIRS)]
MIB = 1 << 20
VMEM = pl.BlockSpec(memory_space=pltpu.VMEM)
SMEM = pl.BlockSpec(memory_space=pltpu.SMEM)
ANY = pl.BlockSpec(memory_space=pl.ANY)
HBM = pl.BlockSpec(memory_space=pltpu.HBM)


def params(mib=52):
    return pltpu.CompilerParams(vmem_limit_bytes=mib * MIB)


def cost(flops, moved):
    return pl.CostEstimate(flops=flops, bytes_accessed=moved, transcendentals=0)


def plane_swap(blocks):
    return lax.all_to_all(blocks, "seq", 0, 0, axis_index_groups=PLANE, tiled=True)


def core_swap(block):
    return lax.ppermute(block, "seq", SWAP)


def head_shift(block, step):
    return lax.ppermute(block, "head", [(i, (i + step) % 4) for i in range(4)])


def exact_dot(a, b):
    return lax.dot_general(a, b, (((1,), (0,)), ((), ())), preferred_element_type=jnp.float32)


def score_dot(a, b):
    return lax.dot_general(a, b, (((1,), (1,)), ((), ())), preferred_element_type=jnp.float32)


def choose_kernel(counts, queries, tokens, out, held, sem):
    @pl.when(lax.axis_index("seq") == 0)
    def _():
        copy = pltpu.make_async_copy(tokens, held, sem)
        copy.start()
        copy.wait()
        row = lax.broadcasted_iota(jnp.int32, out.shape, 0)
        rows = held[...].astype(jnp.float32)
        out[...] = jnp.where(row < counts[0], rows, jnp.nan).astype(out.dtype)

    @pl.when(lax.axis_index("seq") != 0)
    def _():
        copy = pltpu.make_async_copy(queries, out, sem)
        copy.start()
        copy.wait()


def choose(counts, queries, tokens):
    return pl.pallas_call(
        choose_kernel,
        in_specs=[SMEM, ANY, ANY],
        out_specs=VMEM,
        out_shape=jax.ShapeDtypeStruct(tokens.shape, tokens.dtype),
        scratch_shapes=[pltpu.VMEM(tokens.shape, tokens.dtype), pltpu.SemaphoreType.DMA],
        compiler_params=params(4),
        cost_estimate=cost(1000, 2 * MIB),
    )(counts, queries, tokens)


def start_all(copies):
    for copy in copies:
        copy.start()
    return copies


def rows_of(step, size):
    return pl.ds(pl.multiple_of(((lax.axis_index("head") - step + 4) % 4) * size, size), size)


def few_kernel(f0, f1, f2, f3, wq, wk, wv, pack_out, kv_out, held_q, held_kv, sems):
    fews = (f0, f1, f2, f3)
    size = f0.shape[1]
    nk = wk.shape[1]
    copies = []
    for step in range(4):
        rows = rows_of(step, size)
        copies.append(
            start_all(
                [
                    pltpu.make_async_copy(wq.at[rows], held_q.at[step], sems.at[step, 0]),
                    pltpu.make_async_copy(wk.at[rows], held_kv.at[step, 0], sems.at[step, 1]),
                    pltpu.make_async_copy(wv.at[rows], held_kv.at[step, 1], sems.at[step, 2]),
                ]
            )
        )
    q = k = v = 0.0
    for step in range(4):
        for copy in copies[step]:
            copy.wait()
        few = fews[step][...]
        q += exact_dot(few, held_q[step])
        k += exact_dot(few, held_kv[step, 0])
        v += exact_dot(few, held_kv[step, 1])
    slab = f0.shape[0] // 2
    pack = jnp.concatenate([q[:slab], k[slab:], v[slab:]], axis=1)
    pack_out[...] = jnp.broadcast_to(pack[None], pack_out.shape).astype(pack_out.dtype)
    own = jnp.concatenate([k[:slab], v[:slab]], axis=1)
    kv_out[...] = jnp.concatenate([own, jnp.zeros_like(own)], axis=0).astype(kv_out.dtype)


def project_few(fews, w_query, w_key, w_value):
    depth = w_query.shape[0]
    few, size = fews[0].shape
    nq, nk = w_query.shape[1], w_key.shape[1]
    dtype = w_query.dtype
    return pl.pallas_call(
        few_kernel,
        in_specs=[VMEM] * 4 + [HBM] * 3,
        out_specs=[VMEM] * 2,
        out_shape=[
            jax.ShapeDtypeStruct((PAIRS, few // 2, nq + 2 * nk), dtype),
            jax.ShapeDtypeStruct((few, 2 * nk), dtype),
        ],
        scratch_shapes=[
            pltpu.VMEM((4, size, nq), dtype),
            pltpu.VMEM((4, 2, size, nk), dtype),
            pltpu.SemaphoreType.DMA((4, 3)),
        ],
        compiler_params=params(),
        cost_estimate=cost(2 * 128 * depth * (nq + 2 * nk), depth * (nq + 2 * nk) * 2),
    )(*fews, w_query, w_key, w_value)


def chunk_copies(chunk, held, sems, at):
    half = chunk[0].shape[0]
    return [
        pltpu.make_async_copy(part, held.at[pl.ds(i * half, half)], sems.at[at + i])
        for i, part in enumerate(chunk)
    ]


def keys_kernel(*refs):
    (c0, c1, c2a, c2b, c3), (wk, wv, few, out, held, held_kv, acc, sems) = refs[:5], refs[5:]
    count, size = held.shape[1:]
    chunks = (c0,), (c1,), (c2a, c2b), (c3,)
    nk = wk.shape[1]
    copies = []
    for step in range(4):
        rows = rows_of(step, size)
        copies.append(
            start_all(
                [
                    pltpu.make_async_copy(wk.at[rows], held_kv.at[step, 0], sems.at[step, 0]),
                    pltpu.make_async_copy(wv.at[rows], held_kv.at[step, 1], sems.at[step, 1]),
                ]
                + chunk_copies(chunks[step], held.at[step], sems.at[step], 2)
            )
        )
    for step in range(4):
        for copy in copies[step]:
            copy.wait()
        for part in range(2):
            here = pl.ds(part * nk, nk)
            term = exact_dot(held[step], held_kv[step, part])
            if step == 0:
                acc[:, here] = term
            elif step < 3:
                acc[:, here] += term
            else:
                out[:count, here] = (acc[:, here] + term).astype(out.dtype)
    out[count:, :] = few[...]


def project_keys(chunks, w_key, w_value, few):
    rows, size = chunks[0].shape
    nk = w_key.shape[1]
    shape = (rows + few.shape[0], 2 * nk)
    dtype = w_key.dtype
    return pl.pallas_call(
        keys_kernel,
        in_specs=[ANY] * 5 + [HBM] * 2 + [VMEM],
        out_specs=VMEM,
        out_shape=jax.ShapeDtypeStruct(shape, dtype),
        scratch_shapes=[
            pltpu.VMEM((4, rows, size), dtype),
            pltpu.VMEM((4, 2, size, nk), dtype),
            pltpu.VMEM((rows, 2 * nk), jnp.float32),
            pltpu.SemaphoreType.DMA((4, 4)),
        ],
        compiler_params=params(),
        cost_estimate=cost(2 * rows * 4 * size * 2 * nk, 6 * MIB),
    )(*chunks, w_key, w_value, few)


def queries_kernel(*refs):
    (c0, c1, c2a, c2b, c3), (wq, out, held, held_q, acc, sems) = refs[:5], refs[5:]
    count, size = held.shape[1:]
    chunks = (c0,), (c1,), (c2a, c2b), (c3,)
    copies = []
    for step in range(4):
        rows = rows_of(step, size)
        copies.append(
            start_all(
                [
                    pltpu.make_async_copy(wq.at[rows], held_q.at[step], sems.at[step, 0]),
                ]
                + chunk_copies(chunks[step], held.at[step], sems.at[step], 1)
            )
        )
    for step in range(4):
        for copy in copies[step]:
            copy.wait()
        term = exact_dot(held[step], held_q[step])
        if step == 0:
            acc[...] = term
        elif step < 3:
            acc[...] += term
        else:
            out[...] = (acc[...] + term).astype(out.dtype)


def project_queries(chunks, w_query):
    rows, size = chunks[0].shape
    wide = w_query.shape[1]
    dtype = w_query.dtype
    return pl.pallas_call(
        queries_kernel,
        in_specs=[ANY] * 5 + [HBM],
        out_specs=VMEM,
        out_shape=jax.ShapeDtypeStruct((rows, wide), dtype),
        scratch_shapes=[
            pltpu.VMEM((4, rows, size), dtype),
            pltpu.VMEM((4, size, wide), dtype),
            pltpu.VMEM((rows, wide), jnp.float32),
            pltpu.SemaphoreType.DMA((4, 3)),
        ],
        compiler_params=params(),
        cost_estimate=cost(2 * rows * 4 * size * wide, 10 * MIB),
    )(*chunks, w_query)


def query_kernel(counts, sibling, q_ref, mine, other, out):
    seq = lax.axis_index("seq")
    core, pair, count_mine, count_other = seq % 2, seq // 2, counts[0], sibling[0]
    half = q_ref.shape[0]
    blk = 2 * half
    nk = mine.shape[1] // 2
    few = mine.shape[0] - blk
    slab = few // 2
    groups = nk // HD
    heads = (q_ref.shape[1] - 2 * nk) // HD
    local_row = lax.broadcasted_iota(jnp.int32, (half, HD), 0)
    row = local_row + slab * (local_row // slab + core)
    lane = lax.broadcasted_iota(jnp.int32, (half, HD), 1)
    col = lax.broadcasted_iota(jnp.int32, (half, blk), 1)
    first = (2 * pair + core) * slab
    first_other = (2 * pair + 1 - core) * slab
    own_a = (lane < slab) & (first + lane <= row)
    own_b = (lane >= few) & (lane < few + slab) & (first_other + lane - few <= row)
    seen = jnp.concatenate([col < count_mine, col < count_other, own_a | own_b], axis=1)
    fill = jnp.zeros((HD - 2 * few, HD), mine.dtype)
    stats = jnp.zeros((half, HD), jnp.float32)
    for g in range(groups):
        kc, vc = pl.ds(g * HD, HD), pl.ds(nk + g * HD, HD)
        keys, values = (
            jnp.concatenate(
                [mine[:blk, c], other[:blk, c], mine[blk:, c], other[blk:, c], fill], axis=0
            )
            for c in (kc, vc)
        )
        for h in range(g * (heads // groups), (g + 1) * (heads // groups)):
            s = jnp.where(seen, score_dot(q_ref[:, pl.ds(h * HD, HD)], keys), NEG)
            top = jnp.max(s, axis=1, keepdims=True)
            p = jnp.exp2((s - top) * LOG2_SCALE).astype(mine.dtype)
            total = jnp.sum(p.astype(jnp.float32), axis=1, keepdims=True)
            out[:, pl.ds(h * HD, HD)] = exact_dot(p, values)
            stats = jnp.where(lane == h, top, jnp.where(lane == heads + h, total, stats))
    out[:, pl.ds(heads * HD, HD)] = stats


def query_attention(counts, sibling, mine_rows, kv, kv_other):
    rows, wide = mine_rows.shape
    nq = wide - kv.shape[1]
    return pl.pallas_call(
        query_kernel,
        in_specs=[SMEM] * 2 + [VMEM] * 3,
        out_specs=VMEM,
        out_shape=jax.ShapeDtypeStruct((rows, nq + HD), jnp.float32),
        compiler_params=params(24),
        cost_estimate=cost(4 * rows * 640 * nq, 4 * MIB),
    )(counts, sibling, mine_rows, kv, kv_other)


ORDER = (2, 1, 3, 0)


def columns_of(step, size):
    return pl.ds(pl.multiple_of(((lax.axis_index("head") + step) % 4) * size, size), size)


def context_kernel(
    counts, q_ref, kv, a_mine, a_other, w_ref, out0, out1, out2, own, ctx, held, sems
):
    seq, count = lax.axis_index("seq"), counts[0]
    blk = q_ref.shape[0]
    width = own.shape[1]
    nk = kv.shape[1] // 2
    groups = nk // HD
    heads = q_ref.shape[1] // HD
    copies = [
        pltpu.make_async_copy(w_ref.at[:, columns_of(turn, width)], held.at[at], sems.at[at])
        for at, turn in enumerate(ORDER)
    ]
    start_all(copies)
    row = lax.broadcasted_iota(jnp.int32, (blk, blk), 0)
    col = lax.broadcasted_iota(jnp.int32, (blk, blk), 1)
    own_seen = (col <= row) & (col < count)
    front = jnp.zeros((blk, blk), jnp.int32) + seq > 0
    nq = q_ref.shape[1]
    for g in range(groups):
        kc, vc = pl.ds(g * HD, HD), pl.ds(nk + g * HD, HD)
        ac, bc = pl.ds(nq + g * HD, HD), pl.ds(nq + nk + g * HD, HD)
        ka = jnp.concatenate([r[:, ac] for r in (a_mine, a_other)], axis=0)
        va = jnp.concatenate([r[:, bc] for r in (a_mine, a_other)], axis=0)
        va = va.astype(jnp.float32)
        va = jnp.where(va == va, va, 0.0).astype(kv.dtype)
        keys = jnp.concatenate([ka, kv[:blk, kc]], axis=0)
        values = jnp.concatenate([va, kv[:blk, vc]], axis=0)
        seen = None
        for h in range(g * (heads // groups), (g + 1) * (heads // groups)):
            s = score_dot(q_ref[:, pl.ds(h * HD, HD)], keys)
            if seen is None:
                seen = jnp.concatenate([front & (s[:, :blk] == s[:, :blk]), own_seen], axis=1)
            s = jnp.where(seen, s, NEG)
            p = jnp.exp2((s - jnp.max(s, axis=1, keepdims=True)) * LOG2_SCALE)
            p = p * (1.0 / jnp.sum(p, axis=1, keepdims=True))
            ctx[:, pl.ds(h * HD, HD)] = exact_dot(p.astype(kv.dtype), values).astype(ctx.dtype)
    for at in range(4):
        copies[at].wait()
        part = exact_dot(ctx[...], held[at])
        ref = (out0, out1, out2, own)[at]
        ref[...] = part.astype(ref.dtype)


def context(counts, q, kv, a_mine, a_other, w_out):
    blk, nq = q.shape
    depth, wide = w_out.shape
    width = wide // 4
    return pl.pallas_call(
        context_kernel,
        in_specs=[SMEM] + [VMEM] * 4 + [HBM],
        out_specs=[VMEM] * 4,
        out_shape=[jax.ShapeDtypeStruct((blk, width), q.dtype)] * 3
        + [jax.ShapeDtypeStruct((blk, width), jnp.float32)],
        scratch_shapes=[
            pltpu.VMEM((blk, nq), q.dtype),
            pltpu.VMEM((4, depth, width), q.dtype),
            pltpu.SemaphoreType.DMA((4,)),
        ],
        compiler_params=params(),
        cost_estimate=cost(4 * blk * 512 * nq + 2 * blk * depth * wide, 12 * MIB),
    )(counts, q, kv, a_mine, a_other, w_out)


def merge_kernel(parts, w_ref, out0, out1, out2, out3, held, sems):
    width = out0.shape[1]
    heads = (parts.shape[2] - HD) // HD
    copies = [
        pltpu.make_async_copy(w_ref.at[:, columns_of(at, width)], held.at[at], sems.at[at])
        for at in range(4)
    ]
    start_all(copies)
    m = parts[:, :, pl.ds(heads * HD, heads)]
    t = parts[:, :, pl.ds(heads * HD + heads, heads)]
    scale = jnp.exp2((m - jnp.max(m, axis=0, keepdims=True)) * LOG2_SCALE)
    total = jnp.sum(scale * t, axis=0)
    ctx = []
    for h in range(heads):
        o = parts[:, :, pl.ds(h * HD, HD)]
        ctx.append(jnp.sum(scale[:, :, h : h + 1] * o, axis=0) / total[:, h : h + 1])
    ctx = jnp.concatenate(ctx, axis=1).astype(w_ref.dtype)
    for at in range(4):
        copies[at].wait()
        (out0, out1, out2, out3)[at][...] = exact_dot(ctx, held[at])


def merge(parts, w_out):
    slab = parts.shape[1]
    depth, wide = w_out.shape
    width = wide // 4
    return pl.pallas_call(
        merge_kernel,
        in_specs=[VMEM, HBM],
        out_specs=[VMEM] * 4,
        out_shape=[jax.ShapeDtypeStruct((slab, width), jnp.float32)] * 4,
        scratch_shapes=[
            pltpu.VMEM((4, depth, width), w_out.dtype),
            pltpu.SemaphoreType.DMA((4,)),
        ],
        compiler_params=params(),
        cost_estimate=cost(2 * 128 * depth * wide, depth * wide * 2),
    )(parts, w_out)


def total_kernel(a, b, c, d, out):
    total = (a[...] + b[...]) + (c[...] + d[...])
    out[...] = jnp.broadcast_to(total[None], out.shape).astype(out.dtype)


def local(tokens, queries, valid_counts, query_host, w_query, w_key, w_value, w_out):
    host = query_host[0]
    blk, width = tokens.shape
    slab = blk // (2 * PAIRS)
    dtype = tokens.dtype
    half = blk // 2
    right, left = head_shift(tokens, 1), head_shift(tokens, 3)
    sibling = core_swap(valid_counts)

    sent = lax.cond(
        host == 0,
        lambda q, t: choose(valid_counts, core_swap(q), t),
        lambda q, t: choose(valid_counts, q, t),
        queries,
        tokens,
    )
    source = (jnp.maximum(host, 1) * slab).astype(jnp.uint32)
    sent, source = lax.optimization_barrier((sent, source))
    spread = lax.all_to_all(sent, "seq", 0, 0, tiled=True)
    zero = jnp.zeros_like(source)
    picked = jnp.concatenate(
        [lax.dynamic_slice(spread, (source, zero), (slab, width)), spread[:slab]], axis=0
    )
    picked, sibling = lax.optimization_barrier((picked, sibling))
    fews = [picked] + [head_shift(picked, step) for step in (1, 2, 3)]
    right_half, left_half, *fews = lax.optimization_barrier((right[:half], left[half:], *fews))
    chunks = [tokens, right, head_shift(right_half, 1), head_shift(left_half, 3), left]
    pack, few_kv = project_few(fews, w_query, w_key, w_value)
    mine = plane_swap(pack).reshape(blk // 2, -1)
    kv = project_keys(chunks, w_key, w_value, few_kv)
    kv_other = core_swap(kv)
    chunks[0], kv = lax.optimization_barrier((chunks[0], kv))
    q_blk = project_queries(chunks, w_query)
    mine, q_blk = lax.optimization_barrier((mine, q_blk))
    mine_other = core_swap(mine)

    stats = query_attention(valid_counts, sibling, mine, kv, kv_other)
    merged = plane_swap(stats.reshape(PAIRS, slab, -1))
    *partial, own = context(valid_counts, q_blk, kv, mine, mine_other, w_out)
    far, after, before, own = context(valid_counts, q_blk, kv, mine, mine_other, w_out)
    merged, own, after, before, far = lax.optimization_barrier((merged, own, after, before, far))
    term = merge(merged, w_out)
    parts = [term[0]] + [head_shift(term[step], step) for step in (1, 2, 3)]
    after, before, _ = lax.optimization_barrier((after, before, term[0]))
    near = head_shift(after, 1), head_shift(before, 3)
    copies = pl.pallas_call(
        total_kernel,
        out_shape=jax.ShapeDtypeStruct((2 * PAIRS, slab, width), dtype),
        compiler_params=params(24),
    )(*parts)
    far, copies = lax.optimization_barrier((far, copies))
    far = head_shift(far, 2)
    query_out = lax.all_to_all(copies, "seq", 0, 0, tiled=True).reshape(blk, width)
    block_sum = own
    for part in (*near, far):
        block_sum += part.astype(jnp.float32)
    return (block_sum.astype(dtype), query_out)


def solution(mesh):
    return jax.shard_map(
        local,
        mesh=mesh,
        in_specs=(
            P("seq", "head"),
            P("seq", "head"),
            P("seq"),
            P(),
            P(None, "head"),
            P(None, "head"),
            P(None, "head"),
            P("head", None),
        ),
        out_specs=(P("seq", "head"), P(None, "head")),
        check_vma=False,
    )
```

```python
import jax
import jax.numpy as jnp
from jax import lax
from jax.experimental import pallas as pl
from jax.experimental.pallas import tpu as pltpu
from jax.sharding import PartitionSpec as P

HD = 128
LOG2_SCALE = HD ** (-0.5) * 1.4426950408889634
NEG = -1e30
PAIRS = 16
PLANE = [[2 * g + c for g in range(PAIRS)] for c in range(2)]
SWAP = [(i, i ^ 1) for i in range(2 * PAIRS)]
MIB = 1 << 20
VMEM = pl.BlockSpec(memory_space=pltpu.VMEM)
SMEM = pl.BlockSpec(memory_space=pltpu.SMEM)
ANY = pl.BlockSpec(memory_space=pl.ANY)
HBM = pl.BlockSpec(memory_space=pltpu.HBM)


def params(mib=52):
    return pltpu.CompilerParams(vmem_limit_bytes=mib * MIB)


def cost(flops, moved):
    return pl.CostEstimate(flops=flops, bytes_accessed=moved, transcendentals=0)


def plane_swap(blocks):
    return lax.all_to_all(blocks, "seq", 0, 0, axis_index_groups=PLANE, tiled=True)


def core_swap(block):
    return lax.ppermute(block, "seq", SWAP)


def head_shift(block, step):
    return lax.ppermute(block, "head", [(i, (i + step) % 4) for i in range(4)])


def exact_dot(a, b):
    return lax.dot_general(a, b, (((1,), (0,)), ((), ())), preferred_element_type=jnp.float32)


def score_dot(a, b):
    return lax.dot_general(a, b, (((1,), (1,)), ((), ())), preferred_element_type=jnp.float32)


def choose_kernel(counts, queries, tokens, out, held, sem):
    @pl.when(lax.axis_index("seq") == 0)
    def _():
        copy = pltpu.make_async_copy(tokens, held, sem)
        copy.start()
        copy.wait()
        row = lax.broadcasted_iota(jnp.int32, out.shape, 0)
        rows = held[...].astype(jnp.float32)
        out[...] = jnp.where(row < counts[0], rows, jnp.nan).astype(out.dtype)

    @pl.when(lax.axis_index("seq") != 0)
    def _():
        copy = pltpu.make_async_copy(queries, out, sem)
        copy.start()
        copy.wait()


def choose(counts, queries, tokens):
    return pl.pallas_call(
        choose_kernel,
        in_specs=[SMEM, ANY, ANY],
        out_specs=VMEM,
        out_shape=jax.ShapeDtypeStruct(tokens.shape, tokens.dtype),
        scratch_shapes=[pltpu.VMEM(tokens.shape, tokens.dtype), pltpu.SemaphoreType.DMA],
        compiler_params=params(4),
        cost_estimate=cost(1000, 2 * MIB),
    )(counts, queries, tokens)


def start_all(copies):
    for copy in copies:
        copy.start()
    return copies


def rows_of(step, size):
    return pl.ds(pl.multiple_of(((lax.axis_index("head") - step + 4) % 4) * size, size), size)


def few_kernel(fews, wq, wk, wv, pack_out, kv_out, held_q, held_kv, sems):
    size = fews.shape[2]
    nk = wk.shape[1]
    copies = []
    for step in range(4):
        rows = pl.ds(step * size, size)
        copies.append(
            start_all(
                [
                    pltpu.make_async_copy(wq.at[rows], held_q.at[step], sems.at[step, 0]),
                    pltpu.make_async_copy(wk.at[rows], held_kv.at[step, 0], sems.at[step, 1]),
                    pltpu.make_async_copy(wv.at[rows], held_kv.at[step, 1], sems.at[step, 2]),
                ]
            )
        )
    q = k = v = 0.0
    for step in range(4):
        for copy in copies[step]:
            copy.wait()
        few = fews[step]
        q += exact_dot(few, held_q[step])
        k += exact_dot(few, held_kv[step, 0])
        v += exact_dot(few, held_kv[step, 1])
    slab = fews.shape[1] // 2
    pack = jnp.concatenate([q[:slab], k[slab:], v[slab:]], axis=1)
    pack_out[...] = jnp.broadcast_to(pack[None], pack_out.shape).astype(pack_out.dtype)
    own = jnp.concatenate([k[:slab], v[:slab]], axis=1)
    kv_out[...] = jnp.concatenate([own, jnp.zeros_like(own)], axis=0).astype(kv_out.dtype)


def project_few(fews, w_query, w_key, w_value):
    depth = w_query.shape[0]
    few, size = fews.shape[1:]
    nq, nk = w_query.shape[1], w_key.shape[1]
    dtype = w_query.dtype
    return pl.pallas_call(
        few_kernel,
        in_specs=[VMEM] + [HBM] * 3,
        out_specs=[VMEM] * 2,
        out_shape=[
            jax.ShapeDtypeStruct((PAIRS, few // 2, nq + 2 * nk), dtype),
            jax.ShapeDtypeStruct((few, 2 * nk), dtype),
        ],
        scratch_shapes=[
            pltpu.VMEM((4, size, nq), dtype),
            pltpu.VMEM((4, 2, size, nk), dtype),
            pltpu.SemaphoreType.DMA((4, 3)),
        ],
        compiler_params=params(),
        cost_estimate=cost(2 * 128 * depth * (nq + 2 * nk), depth * (nq + 2 * nk) * 2),
    )(fews, w_query, w_key, w_value)


def chunk_copies(chunk, held, sems, at):
    half = chunk[0].shape[0]
    return [
        pltpu.make_async_copy(part, held.at[pl.ds(i * half, half)], sems.at[at + i])
        for i, part in enumerate(chunk)
    ]


def keys_kernel(*refs):
    (c0, c1, c2a, c2b, c3), (wk, wv, few, out, held, held_kv, acc, sems) = refs[:5], refs[5:]
    count, size = held.shape[1:]
    chunks = (c0,), (c1,), (c2a, c2b), (c3,)
    nk = wk.shape[1]
    copies = []
    for step in range(4):
        rows = rows_of(step, size)
        copies.append(
            start_all(
                [
                    pltpu.make_async_copy(wk.at[rows], held_kv.at[step, 0], sems.at[step, 0]),
                    pltpu.make_async_copy(wv.at[rows], held_kv.at[step, 1], sems.at[step, 1]),
                ]
                + chunk_copies(chunks[step], held.at[step], sems.at[step], 2)
            )
        )
    for step in range(4):
        for copy in copies[step]:
            copy.wait()
        for part in range(2):
            here = pl.ds(part * nk, nk)
            term = exact_dot(held[step], held_kv[step, part])
            if step == 0:
                acc[:, here] = term
            elif step < 3:
                acc[:, here] += term
            else:
                out[:count, here] = (acc[:, here] + term).astype(out.dtype)
    out[count:, :] = few[...]


def project_keys(chunks, w_key, w_value, few):
    rows, size = chunks[0].shape
    nk = w_key.shape[1]
    shape = (rows + few.shape[0], 2 * nk)
    dtype = w_key.dtype
    return pl.pallas_call(
        keys_kernel,
        in_specs=[ANY] * 5 + [HBM] * 2 + [VMEM],
        out_specs=VMEM,
        out_shape=jax.ShapeDtypeStruct(shape, dtype),
        scratch_shapes=[
            pltpu.VMEM((4, rows, size), dtype),
            pltpu.VMEM((4, 2, size, nk), dtype),
            pltpu.VMEM((rows, 2 * nk), jnp.float32),
            pltpu.SemaphoreType.DMA((4, 4)),
        ],
        compiler_params=params(),
        cost_estimate=cost(2 * rows * 4 * size * 2 * nk, 6 * MIB),
    )(*chunks, w_key, w_value, few)


def queries_kernel(*refs):
    (c0, c1, c2a, c2b, c3), (wq, out, held, held_q, acc, sems) = refs[:5], refs[5:]
    count, size = held.shape[1:]
    chunks = (c0,), (c1,), (c2a, c2b), (c3,)
    copies = []
    for step in range(4):
        rows = rows_of(step, size)
        copies.append(
            start_all(
                [
                    pltpu.make_async_copy(wq.at[rows], held_q.at[step], sems.at[step, 0]),
                ]
                + chunk_copies(chunks[step], held.at[step], sems.at[step], 1)
            )
        )
    for step in range(4):
        for copy in copies[step]:
            copy.wait()
        term = exact_dot(held[step], held_q[step])
        if step == 0:
            acc[...] = term
        elif step < 3:
            acc[...] += term
        else:
            out[...] = (acc[...] + term).astype(out.dtype)


def project_queries(chunks, w_query):
    rows, size = chunks[0].shape
    wide = w_query.shape[1]
    dtype = w_query.dtype
    return pl.pallas_call(
        queries_kernel,
        in_specs=[ANY] * 5 + [HBM],
        out_specs=VMEM,
        out_shape=jax.ShapeDtypeStruct((rows, wide), dtype),
        scratch_shapes=[
            pltpu.VMEM((4, rows, size), dtype),
            pltpu.VMEM((4, size, wide), dtype),
            pltpu.VMEM((rows, wide), jnp.float32),
            pltpu.SemaphoreType.DMA((4, 3)),
        ],
        compiler_params=params(),
        cost_estimate=cost(2 * rows * 4 * size * wide, 10 * MIB),
    )(*chunks, w_query)


def split(x):
    high = x.astype(jnp.bfloat16).astype(jnp.float32)
    middle = (x - high).astype(jnp.bfloat16).astype(jnp.float32)
    return [high, middle, x - high - middle]


def query_kernel(counts, sibling, q_ref, mine, other, out):
    seq = lax.axis_index("seq")
    core, pair, count_mine, count_other = seq % 2, seq // 2, counts[0], sibling[0]
    half = q_ref.shape[0]
    blk = 2 * half
    nk = mine.shape[1] // 2
    few = mine.shape[0] - blk
    slab = few // 2
    groups = nk // HD
    heads = (q_ref.shape[1] - 2 * nk) // HD
    local_row = lax.broadcasted_iota(jnp.int32, (HD, 2 * half), 1) % half
    row = local_row + slab * (local_row // slab + core)
    key = lax.broadcasted_iota(jnp.int32, (HD, 2 * half), 0)
    first = (2 * pair + core) * slab
    first_other = (2 * pair + 1 - core) * slab
    own_a = (key < slab) & (first + key <= row)
    own_b = (key >= few) & (key < few + slab) & (first_other + key - few <= row)
    block_key = lax.broadcasted_iota(jnp.int32, (blk, 2 * half), 0)
    seen = jnp.concatenate([block_key < count_mine, block_key < count_other, own_a | own_b], axis=0)
    fill = jnp.zeros((HD - 2 * few, HD), mine.dtype)
    tops, totals = [], []
    for g in range(groups):
        keys, values = (
            jnp.concatenate(
                [mine[:blk, c], other[:blk, c], mine[blk:, c], other[blk:, c], fill], axis=0
            )
            for c in (pl.ds(g * HD, HD), pl.ds(nk + g * HD, HD))
        )
        values = values.T
        for h in range(g * (heads // groups), (g + 1) * (heads // groups), 2):
            q = jnp.concatenate([q_ref[:, pl.ds((h + i) * HD, HD)] for i in range(2)], axis=0)
            s = jnp.where(seen, score_dot(keys, q), NEG)
            top = jnp.max(s, axis=0, keepdims=True)
            p = jnp.exp2((s - top) * LOG2_SCALE).astype(mine.dtype)
            total = jnp.sum(p.astype(jnp.float32), axis=0, keepdims=True)
            o = exact_dot(values, p).T.astype(out.dtype)
            for i in range(2):
                out[:, pl.ds((h + i) * HD, HD)] = o[i * half : (i + 1) * half]
                tops.append(top[:, i * half : (i + 1) * half])
                totals.append(total[:, i * half : (i + 1) * half])
    stats = [part for x in (tops, totals) for part in split(jnp.concatenate(x, axis=0))]
    pad = jnp.zeros((HD - 6 * heads, half), jnp.float32)
    out[:, pl.ds(heads * HD, HD)] = jnp.concatenate(stats + [pad], axis=0).T.astype(out.dtype)


def query_attention(counts, sibling, mine_rows, kv, kv_other):
    rows, wide = mine_rows.shape
    nq = wide - kv.shape[1]
    return pl.pallas_call(
        query_kernel,
        in_specs=[SMEM] * 2 + [VMEM] * 3,
        out_specs=VMEM,
        out_shape=jax.ShapeDtypeStruct((rows, nq + HD), kv.dtype),
        compiler_params=params(24),
        cost_estimate=cost(4 * rows * 640 * nq, 4 * MIB),
    )(counts, sibling, mine_rows, kv, kv_other)


ORDER = (2, 1, 3, 0)


def columns_of(step, size):
    return pl.ds(pl.multiple_of(((lax.axis_index("head") + step) % 4) * size, size), size)


def context_kernel(
    counts, q_ref, kv, a_mine, a_other, w_ref, out0, out1, out2, own, ctx, held, sems
):
    seq, count = lax.axis_index("seq"), counts[0]
    blk = q_ref.shape[0]
    width = own.shape[1]
    nk = kv.shape[1] // 2
    groups = nk // HD
    heads = q_ref.shape[1] // HD
    copies = [
        pltpu.make_async_copy(w_ref.at[:, columns_of(turn, width)], held.at[at], sems.at[at])
        for at, turn in enumerate(ORDER)
    ]
    start_all(copies)
    key = lax.broadcasted_iota(jnp.int32, (blk, blk), 0)
    row = lax.broadcasted_iota(jnp.int32, (blk, blk), 1)
    own_seen = (key <= row) & (key < count)
    front = jnp.zeros((blk, blk), jnp.int32) + seq > 0
    nq = q_ref.shape[1]
    for g in range(groups):
        kc, vc = pl.ds(g * HD, HD), pl.ds(nk + g * HD, HD)
        ac, bc = pl.ds(nq + g * HD, HD), pl.ds(nq + nk + g * HD, HD)
        ka = jnp.concatenate([r[:, ac] for r in (a_mine, a_other)], axis=0)
        va = jnp.concatenate([r[:, bc] for r in (a_mine, a_other)], axis=0)
        va = va.astype(jnp.float32)
        va = jnp.where(va == va, va, 0.0).astype(kv.dtype)
        keys = jnp.concatenate([ka, kv[:blk, kc]], axis=0)
        values = jnp.concatenate([va, kv[:blk, vc]], axis=0).T
        seen = None
        for h in range(g * (heads // groups), (g + 1) * (heads // groups)):
            s = score_dot(keys, q_ref[:, pl.ds(h * HD, HD)])
            if seen is None:
                seen = jnp.concatenate([front & (s[:blk] == s[:blk]), own_seen], axis=0)
            s = jnp.where(seen, s, NEG)
            p = jnp.exp2((s - jnp.max(s, axis=0, keepdims=True)) * LOG2_SCALE)
            p = p * (1.0 / jnp.sum(p, axis=0, keepdims=True))
            ctx[:, pl.ds(h * HD, HD)] = exact_dot(values, p.astype(kv.dtype)).T.astype(ctx.dtype)
    for at in range(4):
        copies[at].wait()
        part = exact_dot(ctx[...], held[at])
        ref = (out0, out1, out2, own)[at]
        ref[...] = part.astype(ref.dtype)


def context(counts, q, kv, a_mine, a_other, w_out):
    blk, nq = q.shape
    depth, wide = w_out.shape
    width = wide // 4
    return pl.pallas_call(
        context_kernel,
        in_specs=[SMEM] + [VMEM] * 4 + [HBM],
        out_specs=[VMEM] * 4,
        out_shape=[jax.ShapeDtypeStruct((blk, width), q.dtype)] * 3
        + [jax.ShapeDtypeStruct((blk, width), jnp.float32)],
        scratch_shapes=[
            pltpu.VMEM((blk, nq), q.dtype),
            pltpu.VMEM((4, depth, width), q.dtype),
            pltpu.SemaphoreType.DMA((4,)),
        ],
        compiler_params=params(),
        cost_estimate=cost(4 * blk * 512 * nq + 2 * blk * depth * wide, 12 * MIB),
    )(counts, q, kv, a_mine, a_other, w_out)


def merge_kernel(parts, w_ref, out0, out1, out2, out3, held, sems):
    width = out0.shape[1]
    heads = (parts.shape[2] - HD) // HD
    copies = [
        pltpu.make_async_copy(w_ref.at[:, columns_of(at, width)], held.at[at], sems.at[at])
        for at in range(4)
    ]
    start_all(copies)
    stats = parts[:, :, pl.ds(heads * HD, HD)].astype(jnp.float32)
    stats = [stats[:, :, i * heads : (i + 1) * heads] for i in range(6)]
    m = stats[0] + stats[1] + stats[2]
    t = stats[3] + stats[4] + stats[5]
    scale = jnp.exp2((m - jnp.max(m, axis=0, keepdims=True)) * LOG2_SCALE)
    total = jnp.sum(scale * t, axis=0)
    ctx = []
    for h in range(heads):
        o = parts[:, :, pl.ds(h * HD, HD)].astype(jnp.float32)
        ctx.append(jnp.sum(scale[:, :, h : h + 1] * o, axis=0) / total[:, h : h + 1])
    ctx = jnp.concatenate(ctx, axis=1).astype(w_ref.dtype)
    for at in range(4):
        copies[at].wait()
        (out0, out1, out2, out3)[at][...] = exact_dot(ctx, held[at])


def merge(parts, w_out):
    slab = parts.shape[1]
    depth, wide = w_out.shape
    width = wide // 4
    return pl.pallas_call(
        merge_kernel,
        in_specs=[VMEM, HBM],
        out_specs=[VMEM] * 4,
        out_shape=[jax.ShapeDtypeStruct((slab, width), jnp.float32)] * 4,
        scratch_shapes=[
            pltpu.VMEM((4, depth, width), w_out.dtype),
            pltpu.SemaphoreType.DMA((4,)),
        ],
        compiler_params=params(),
        cost_estimate=cost(2 * 128 * depth * wide, depth * wide * 2),
    )(parts, w_out)


def total_kernel(a, b, c, d, out):
    total = (a[...] + b[...]) + (c[...] + d[...])
    out[...] = jnp.broadcast_to(total[None], out.shape).astype(out.dtype)


def local(tokens, queries, valid_counts, query_host, w_query, w_key, w_value, w_out):
    host = query_host[0]
    blk, width = tokens.shape
    slab = blk // (2 * PAIRS)
    dtype = tokens.dtype
    half = blk // 2
    right, left = head_shift(tokens, 1), head_shift(tokens, 3)
    sibling = core_swap(valid_counts)

    sent = lax.cond(
        host == 0,
        lambda q, t: choose(valid_counts, core_swap(q), t),
        lambda q, t: choose(valid_counts, q, t),
        queries,
        tokens,
    )
    source = (jnp.maximum(host, 1) * slab).astype(jnp.uint32)
    sent, source = lax.optimization_barrier((sent, source))
    spread = lax.all_to_all(sent, "seq", 0, 0, tiled=True)
    zero = jnp.zeros_like(source)
    picked = jnp.concatenate(
        [lax.dynamic_slice(spread, (source, zero), (slab, width)), spread[:slab]], axis=0
    )
    picked, sibling = lax.optimization_barrier((picked, sibling))
    copies = jnp.broadcast_to(picked[None], (4,) + picked.shape)
    fews = lax.all_to_all(copies, "head", 0, 0, tiled=True)
    right_half, left_half, _ = lax.optimization_barrier((right[:half], left[half:], picked))
    chunks = [tokens, right, head_shift(right_half, 1), head_shift(left_half, 3), left]
    pack, few_kv = project_few(fews, w_query, w_key, w_value)
    mine = plane_swap(pack).reshape(blk // 2, -1)
    kv = project_keys(chunks, w_key, w_value, few_kv)
    kv_other = core_swap(kv)
    chunks[0], kv = lax.optimization_barrier((chunks[0], kv))
    q_blk = project_queries(chunks, w_query)
    mine, q_blk = lax.optimization_barrier((mine, q_blk))
    mine_other = core_swap(mine)

    stats = query_attention(valid_counts, sibling, mine, kv, kv_other)
    merged = plane_swap(stats.reshape(PAIRS, slab, -1))
    *partial, own = context(valid_counts, q_blk, kv, mine, mine_other, w_out)
    far, after, before, own = context(valid_counts, q_blk, kv, mine, mine_other, w_out)
    merged, own, before, far = lax.optimization_barrier((merged, own, before, far))
    term = merge(merged, w_out)
    parts = [term[0]] + [head_shift(term[step], step) for step in (1, 2, 3)]
    before, _ = lax.optimization_barrier((before, term[0]))
    near = head_shift(after, 1), head_shift(before, 3)
    copies = pl.pallas_call(
        total_kernel,
        out_shape=jax.ShapeDtypeStruct((2 * PAIRS, slab, width), dtype),
        compiler_params=params(24),
    )(*parts)
    far, copies = lax.optimization_barrier((far, copies))
    far = head_shift(far, 2)
    query_out = lax.all_to_all(copies, "seq", 0, 0, tiled=True).reshape(blk, width)
    block_sum = own
    for part in (*near, far):
        block_sum += part.astype(jnp.float32)
    return (block_sum.astype(dtype), query_out)


def solution(mesh):
    return jax.shard_map(
        local,
        mesh=mesh,
        in_specs=(
            P("seq", "head"),
            P("seq", "head"),
            P("seq"),
            P(),
            P(None, "head"),
            P(None, "head"),
            P(None, "head"),
            P("head", None),
        ),
        out_specs=(P("seq", "head"), P(None, "head")),
        check_vma=False,
    )
```

```python
import jax
import jax.numpy as jnp
from jax import lax
from jax.experimental import pallas as pl
from jax.experimental.pallas import tpu as pltpu
from jax.sharding import PartitionSpec as P

HD = 128
LOG2_SCALE = HD ** (-0.5) * 1.4426950408889634
NEG = -1e30
PAIRS = 16
PLANE = [[2 * g + c for g in range(PAIRS)] for c in range(2)]
SWAP = [(i, i ^ 1) for i in range(2 * PAIRS)]
MIB = 1 << 20
VMEM = pl.BlockSpec(memory_space=pltpu.VMEM)
SMEM = pl.BlockSpec(memory_space=pltpu.SMEM)
ANY = pl.BlockSpec(memory_space=pl.ANY)
HBM = pl.BlockSpec(memory_space=pltpu.HBM)


def params(mib=52):
    return pltpu.CompilerParams(vmem_limit_bytes=mib * MIB)


def cost(flops, moved):
    return pl.CostEstimate(flops=flops, bytes_accessed=moved, transcendentals=0)


def plane_swap(blocks):
    return lax.all_to_all(blocks, "seq", 0, 0, axis_index_groups=PLANE, tiled=True)


def core_swap(block):
    return lax.ppermute(block, "seq", SWAP)


def head_shift(block, step):
    return lax.ppermute(block, "head", [(i, (i + step) % 4) for i in range(4)])


def exact_dot(a, b):
    return lax.dot_general(a, b, (((1,), (0,)), ((), ())), preferred_element_type=jnp.float32)


def score_dot(a, b):
    return lax.dot_general(a, b, (((1,), (1,)), ((), ())), preferred_element_type=jnp.float32)


def choose_kernel(counts, queries, tokens, out, held, sem):
    @pl.when(lax.axis_index("seq") == 0)
    def _():
        copy = pltpu.make_async_copy(tokens, held, sem)
        copy.start()
        copy.wait()
        row = lax.broadcasted_iota(jnp.int32, out.shape, 0)
        rows = held[...].astype(jnp.float32)
        out[...] = jnp.where(row < counts[0], rows, jnp.nan).astype(out.dtype)

    @pl.when(lax.axis_index("seq") != 0)
    def _():
        copy = pltpu.make_async_copy(queries, out, sem)
        copy.start()
        copy.wait()


def choose(counts, queries, tokens):
    return pl.pallas_call(
        choose_kernel,
        in_specs=[SMEM, ANY, ANY],
        out_specs=VMEM,
        out_shape=jax.ShapeDtypeStruct(tokens.shape, tokens.dtype),
        scratch_shapes=[pltpu.VMEM(tokens.shape, tokens.dtype), pltpu.SemaphoreType.DMA],
        compiler_params=params(4),
        cost_estimate=cost(1000, 2 * MIB),
    )(counts, queries, tokens)


def start_all(copies):
    for copy in copies:
        copy.start()
    return copies


def rows_of(step, size):
    return pl.ds(pl.multiple_of(((lax.axis_index("head") - step + 4) % 4) * size, size), size)


def few_kernel(fews, wq, wk, wv, pack_out, kv_out, held_q, held_kv, sems):
    size = fews.shape[2]
    nk = wk.shape[1]
    copies = []
    for step in range(4):
        rows = pl.ds(step * size, size)
        copies.append(
            start_all(
                [
                    pltpu.make_async_copy(wq.at[rows], held_q.at[step], sems.at[step, 0]),
                    pltpu.make_async_copy(wk.at[rows], held_kv.at[step, 0], sems.at[step, 1]),
                    pltpu.make_async_copy(wv.at[rows], held_kv.at[step, 1], sems.at[step, 2]),
                ]
            )
        )
    q = k = v = 0.0
    for step in range(4):
        for copy in copies[step]:
            copy.wait()
        few = fews[step]
        q += exact_dot(few, held_q[step])
        k += exact_dot(few, held_kv[step, 0])
        v += exact_dot(few, held_kv[step, 1])
    slab = fews.shape[1] // 2
    pack = jnp.concatenate([q[:slab], k[slab:], v[slab:]], axis=1)
    pack_out[...] = jnp.broadcast_to(pack[None], pack_out.shape).astype(pack_out.dtype)
    own = jnp.concatenate([k[:slab], v[:slab]], axis=1)
    kv_out[...] = jnp.concatenate([own, jnp.zeros_like(own)], axis=0).astype(kv_out.dtype)


def project_few(fews, w_query, w_key, w_value):
    depth = w_query.shape[0]
    few, size = fews.shape[1:]
    nq, nk = w_query.shape[1], w_key.shape[1]
    dtype = w_query.dtype
    return pl.pallas_call(
        few_kernel,
        in_specs=[VMEM] + [HBM] * 3,
        out_specs=[VMEM] * 2,
        out_shape=[
            jax.ShapeDtypeStruct((PAIRS, few // 2, nq + 2 * nk), dtype),
            jax.ShapeDtypeStruct((few, 2 * nk), dtype),
        ],
        scratch_shapes=[
            pltpu.VMEM((4, size, nq), dtype),
            pltpu.VMEM((4, 2, size, nk), dtype),
            pltpu.SemaphoreType.DMA((4, 3)),
        ],
        compiler_params=params(),
        cost_estimate=cost(2 * 128 * depth * (nq + 2 * nk), depth * (nq + 2 * nk) * 2),
    )(fews, w_query, w_key, w_value)


def chunk_copies(chunk, held, sems, at):
    half = chunk[0].shape[0]
    return [
        pltpu.make_async_copy(part, held.at[pl.ds(i * half, half)], sems.at[at + i])
        for i, part in enumerate(chunk)
    ]


def keys_kernel(*refs):
    (c0, c1, c2a, c2b, c3), (wk, wv, few, out, held, held_kv, acc, sems) = refs[:5], refs[5:]
    count, size = held.shape[1:]
    chunks = (c0,), (c1,), (c2a, c2b), (c3,)
    nk = wk.shape[1]
    copies = []
    for step in range(4):
        rows = rows_of(step, size)
        copies.append(
            start_all(
                [
                    pltpu.make_async_copy(wk.at[rows], held_kv.at[step, 0], sems.at[step, 0]),
                    pltpu.make_async_copy(wv.at[rows], held_kv.at[step, 1], sems.at[step, 1]),
                ]
                + chunk_copies(chunks[step], held.at[step], sems.at[step], 2)
            )
        )
    for step in range(4):
        for copy in copies[step]:
            copy.wait()
        for part in range(2):
            here = pl.ds(part * nk, nk)
            term = exact_dot(held[step], held_kv[step, part])
            if step == 0:
                acc[:, here] = term
            elif step < 3:
                acc[:, here] += term
            else:
                out[:count, here] = (acc[:, here] + term).astype(out.dtype)
    out[count:, :] = few[...]


def project_keys(chunks, w_key, w_value, few):
    rows, size = chunks[0].shape
    nk = w_key.shape[1]
    shape = (rows + few.shape[0], 2 * nk)
    dtype = w_key.dtype
    return pl.pallas_call(
        keys_kernel,
        in_specs=[ANY] * 5 + [HBM] * 2 + [VMEM],
        out_specs=VMEM,
        out_shape=jax.ShapeDtypeStruct(shape, dtype),
        scratch_shapes=[
            pltpu.VMEM((4, rows, size), dtype),
            pltpu.VMEM((4, 2, size, nk), dtype),
            pltpu.VMEM((rows, 2 * nk), jnp.float32),
            pltpu.SemaphoreType.DMA((4, 4)),
        ],
        compiler_params=params(),
        cost_estimate=cost(2 * rows * 4 * size * 2 * nk, 6 * MIB),
    )(*chunks, w_key, w_value, few)


def queries_kernel(*refs):
    (c0, c1, c2a, c2b, c3), (wq, out, held, held_q, acc, sems) = refs[:5], refs[5:]
    count, size = held.shape[1:]
    chunks = (c0,), (c1,), (c2a, c2b), (c3,)
    copies = []
    for step in range(4):
        rows = rows_of(step, size)
        copies.append(
            start_all(
                [
                    pltpu.make_async_copy(wq.at[rows], held_q.at[step], sems.at[step, 0]),
                ]
                + chunk_copies(chunks[step], held.at[step], sems.at[step], 1)
            )
        )
    for step in range(4):
        for copy in copies[step]:
            copy.wait()
        term = exact_dot(held[step], held_q[step])
        if step == 0:
            acc[...] = term
        elif step < 3:
            acc[...] += term
        else:
            out[...] = (acc[...] + term).astype(out.dtype)


def project_queries(chunks, w_query):
    rows, size = chunks[0].shape
    wide = w_query.shape[1]
    dtype = w_query.dtype
    return pl.pallas_call(
        queries_kernel,
        in_specs=[ANY] * 5 + [HBM],
        out_specs=VMEM,
        out_shape=jax.ShapeDtypeStruct((rows, wide), dtype),
        scratch_shapes=[
            pltpu.VMEM((4, rows, size), dtype),
            pltpu.VMEM((4, size, wide), dtype),
            pltpu.VMEM((rows, wide), jnp.float32),
            pltpu.SemaphoreType.DMA((4, 3)),
        ],
        compiler_params=params(),
        cost_estimate=cost(2 * rows * 4 * size * wide, 10 * MIB),
    )(*chunks, w_query)


def split(x):
    high = x.astype(jnp.bfloat16).astype(jnp.float32)
    middle = (x - high).astype(jnp.bfloat16).astype(jnp.float32)
    return [high, middle, x - high - middle]


def query_kernel(counts, sibling, q_ref, mine, other, out):
    seq = lax.axis_index("seq")
    core, pair, count_mine, count_other = seq % 2, seq // 2, counts[0], sibling[0]
    half = q_ref.shape[0]
    blk = 2 * half
    nk = mine.shape[1] // 2
    few = mine.shape[0] - blk
    slab = few // 2
    groups = nk // HD
    heads = (q_ref.shape[1] - 2 * nk) // HD
    local_row = lax.broadcasted_iota(jnp.int32, (HD, 2 * half), 1) % half
    row = local_row + slab * (local_row // slab + core)
    key = lax.broadcasted_iota(jnp.int32, (HD, 2 * half), 0)
    first = (2 * pair + core) * slab
    first_other = (2 * pair + 1 - core) * slab
    own_a = (key < slab) & (first + key <= row)
    own_b = (key >= few) & (key < few + slab) & (first_other + key - few <= row)
    block_key = lax.broadcasted_iota(jnp.int32, (blk, 2 * half), 0)
    seen = jnp.concatenate([block_key < count_mine, block_key < count_other, own_a | own_b], axis=0)
    fill = jnp.zeros((HD - 2 * few, HD), mine.dtype)
    tops, totals = [], []
    for g in range(groups):
        keys, values = (
            jnp.concatenate(
                [mine[:blk, c], other[:blk, c], mine[blk:, c], other[blk:, c], fill], axis=0
            )
            for c in (pl.ds(g * HD, HD), pl.ds(nk + g * HD, HD))
        )
        values = values.T
        for h in range(g * (heads // groups), (g + 1) * (heads // groups), 2):
            q = jnp.concatenate([q_ref[:, pl.ds((h + i) * HD, HD)] for i in range(2)], axis=0)
            s = jnp.where(seen, score_dot(keys, q), NEG)
            top = jnp.max(s, axis=0, keepdims=True)
            p = jnp.exp2((s - top) * LOG2_SCALE).astype(mine.dtype)
            total = jnp.sum(p.astype(jnp.float32), axis=0, keepdims=True)
            o = exact_dot(values, p).T.astype(out.dtype)
            for i in range(2):
                out[:, pl.ds((h + i) * HD, HD)] = o[i * half : (i + 1) * half]
                tops.append(top[:, i * half : (i + 1) * half])
                totals.append(total[:, i * half : (i + 1) * half])
    stats = [part for x in (tops, totals) for part in split(jnp.concatenate(x, axis=0))]
    pad = jnp.zeros((HD - 6 * heads, half), jnp.float32)
    out[:, pl.ds(heads * HD, HD)] = jnp.concatenate(stats + [pad], axis=0).T.astype(out.dtype)


def query_attention(counts, sibling, mine_rows, kv, kv_other):
    rows, wide = mine_rows.shape
    nq = wide - kv.shape[1]
    return pl.pallas_call(
        query_kernel,
        in_specs=[SMEM] * 2 + [VMEM] * 3,
        out_specs=VMEM,
        out_shape=jax.ShapeDtypeStruct((rows, nq + HD), kv.dtype),
        compiler_params=params(24),
        cost_estimate=cost(4 * rows * 640 * nq, 4 * MIB),
    )(counts, sibling, mine_rows, kv, kv_other)


ORDER = (2, 1, 3, 0)


def columns_of(step, size):
    return pl.ds(pl.multiple_of(((lax.axis_index("head") + step) % 4) * size, size), size)


def context_kernel(
    counts, q_ref, kv, a_mine, a_other, w_ref, out0, out1, out2, own, ctx, held, sems
):
    seq, count = lax.axis_index("seq"), counts[0]
    blk = q_ref.shape[0]
    width = own.shape[1]
    nk = kv.shape[1] // 2
    groups = nk // HD
    heads = q_ref.shape[1] // HD
    copies = [
        pltpu.make_async_copy(w_ref.at[:, columns_of(turn, width)], held.at[at], sems.at[at])
        for at, turn in enumerate(ORDER)
    ]
    start_all(copies)
    half = blk // 2
    key = lax.broadcasted_iota(jnp.int32, (blk, blk), 0)
    row = lax.broadcasted_iota(jnp.int32, (blk, blk), 1) % half
    own_seen = [(key <= row + at * half) & (key < count) for at in range(2)]
    front = jnp.zeros((blk, blk), jnp.int32) + seq > 0
    nq = q_ref.shape[1]
    for g in range(groups):
        kc, vc = pl.ds(g * HD, HD), pl.ds(nk + g * HD, HD)
        ac, bc = pl.ds(nq + g * HD, HD), pl.ds(nq + nk + g * HD, HD)
        ka = jnp.concatenate([a_mine[:, ac], a_other[:, kc]], axis=0)
        va = jnp.concatenate([a_mine[:, bc], a_other[:, vc]], axis=0)
        va = va.astype(jnp.float32)
        va = jnp.where(va == va, va, 0.0).astype(kv.dtype)
        keys = jnp.concatenate([ka, kv[:blk, kc]], axis=0)
        values = jnp.concatenate([va, kv[:blk, vc]], axis=0).T
        valid = None
        for h in range(g * (heads // groups), (g + 1) * (heads // groups), 2):
            for at in range(2):
                rows = pl.ds(at * half, half)
                size = blk + (at + 1) * half
                q = jnp.concatenate([q_ref[rows, pl.ds((h + i) * HD, HD)] for i in range(2)], axis=0)
                s = score_dot(keys[:size], q)
                if valid is None:
                    valid = front & (s[:blk] == s[:blk])
                seen = jnp.concatenate([valid, own_seen[at][: size - blk]], axis=0)
                s = jnp.where(seen, s, NEG)
                p = jnp.exp2((s - jnp.max(s, axis=0, keepdims=True)) * LOG2_SCALE)
                p = p * (1.0 / jnp.sum(p, axis=0, keepdims=True))
                o = exact_dot(values[:, :size], p.astype(kv.dtype)).T.astype(ctx.dtype)
                for i in range(2):
                    ctx[rows, pl.ds((h + i) * HD, HD)] = o[i * half : (i + 1) * half]
    for at in range(4):
        copies[at].wait()
        part = exact_dot(ctx[...], held[at])
        ref = (out0, out1, out2, own)[at]
        ref[...] = part.astype(ref.dtype)


def context(counts, q, kv, a_mine, a_other, w_out):
    blk, nq = q.shape
    depth, wide = w_out.shape
    width = wide // 4
    return pl.pallas_call(
        context_kernel,
        in_specs=[SMEM] + [VMEM] * 4 + [HBM],
        out_specs=[VMEM] * 4,
        out_shape=[jax.ShapeDtypeStruct((blk, width), q.dtype)] * 3
        + [jax.ShapeDtypeStruct((blk, width), jnp.float32)],
        scratch_shapes=[
            pltpu.VMEM((blk, nq), q.dtype),
            pltpu.VMEM((4, depth, width), q.dtype),
            pltpu.SemaphoreType.DMA((4,)),
        ],
        compiler_params=params(),
        cost_estimate=cost(4 * blk * 512 * nq + 2 * blk * depth * wide, 12 * MIB),
    )(counts, q, kv, a_mine, a_other, w_out)


def merge_kernel(parts, w_ref, out0, out1, out2, out3, held, sems):
    width = out0.shape[1]
    heads = (parts.shape[2] - HD) // HD
    copies = [
        pltpu.make_async_copy(w_ref.at[:, columns_of(at, width)], held.at[at], sems.at[at])
        for at in range(4)
    ]
    start_all(copies)
    stats = parts[:, :, pl.ds(heads * HD, HD)].astype(jnp.float32)
    stats = [stats[:, :, i * heads : (i + 1) * heads] for i in range(6)]
    m = stats[0] + stats[1] + stats[2]
    t = stats[3] + stats[4] + stats[5]
    scale = jnp.exp2((m - jnp.max(m, axis=0, keepdims=True)) * LOG2_SCALE)
    total = jnp.sum(scale * t, axis=0)
    ctx = []
    for h in range(heads):
        o = parts[:, :, pl.ds(h * HD, HD)].astype(jnp.float32)
        ctx.append(jnp.sum(scale[:, :, h : h + 1] * o, axis=0) / total[:, h : h + 1])
    ctx = jnp.concatenate(ctx, axis=1).astype(w_ref.dtype)
    for at in range(4):
        copies[at].wait()
        (out0, out1, out2, out3)[at][...] = exact_dot(ctx, held[at])


def merge(parts, w_out):
    slab = parts.shape[1]
    depth, wide = w_out.shape
    width = wide // 4
    return pl.pallas_call(
        merge_kernel,
        in_specs=[VMEM, HBM],
        out_specs=[VMEM] * 4,
        out_shape=[jax.ShapeDtypeStruct((slab, width), jnp.float32)] * 4,
        scratch_shapes=[
            pltpu.VMEM((4, depth, width), w_out.dtype),
            pltpu.SemaphoreType.DMA((4,)),
        ],
        compiler_params=params(),
        cost_estimate=cost(2 * 128 * depth * wide, depth * wide * 2),
    )(parts, w_out)


def total_kernel(a, b, c, d, out):
    total = (a[...] + b[...]) + (c[...] + d[...])
    total = jnp.concatenate([total, total], axis=0).astype(out.dtype)
    for at in range(0, out.shape[0], total.shape[0]):
        out[pl.ds(at, total.shape[0]), :] = total


def local(tokens, queries, valid_counts, query_host, w_query, w_key, w_value, w_out):
    host = query_host[0]
    blk, width = tokens.shape
    slab = blk // (2 * PAIRS)
    dtype = tokens.dtype
    half = blk // 2
    right, left = head_shift(tokens, 1), head_shift(tokens, 3)
    sibling = core_swap(valid_counts)

    sent = lax.cond(
        host == 0,
        lambda q, t: choose(valid_counts, core_swap(q), t),
        lambda q, t: choose(valid_counts, q, t),
        queries,
        tokens,
    )
    source = (jnp.maximum(host, 1) * slab).astype(jnp.uint32)
    sent, source = lax.optimization_barrier((sent, source))
    spread = lax.all_to_all(sent, "seq", 0, 0, tiled=True)
    zero = jnp.zeros_like(source)
    picked = jnp.concatenate(
        [lax.dynamic_slice(spread, (source, zero), (slab, width)), spread[:slab]], axis=0
    )
    picked, sibling = lax.optimization_barrier((picked, sibling))
    copies = jnp.broadcast_to(picked[None], (4,) + picked.shape)
    fews = lax.all_to_all(copies, "head", 0, 0, tiled=True)
    right_half, left_half, _ = lax.optimization_barrier((right[:half], left[half:], picked))
    chunks = [tokens, right, head_shift(right_half, 1), head_shift(left_half, 3), left]
    pack, few_kv = project_few(fews, w_query, w_key, w_value)
    mine = plane_swap(pack).reshape(blk // 2, -1)
    kv = project_keys(chunks, w_key, w_value, few_kv)
    kv_other = core_swap(kv)
    chunks[0], kv = lax.optimization_barrier((chunks[0], kv))
    q_blk = project_queries(chunks, w_query)
    mine, q_blk = lax.optimization_barrier((mine, q_blk))
    mine_other = core_swap(mine[:, w_query.shape[1] :])

    stats = query_attention(valid_counts, sibling, mine, kv, kv_other)
    merged = plane_swap(stats.reshape(PAIRS, slab, -1))
    *partial, own = context(valid_counts, q_blk, kv, mine, mine_other, w_out)
    far, after, before, own = context(valid_counts, q_blk, kv, mine, mine_other, w_out)
    merged, own, before, far = lax.optimization_barrier((merged, own, before, far))
    term = merge(merged, w_out)
    parts = [term[0]] + [head_shift(term[step], step) for step in (1, 2, 3)]
    before, _ = lax.optimization_barrier((before, term[0]))
    near = head_shift(after, 1), head_shift(before, 3)
    copies = pl.pallas_call(
        total_kernel,
        out_shape=jax.ShapeDtypeStruct((blk, width), dtype),
        compiler_params=params(24),
    )(*parts)
    far, copies = lax.optimization_barrier((far, copies))
    far = head_shift(far, 2)
    query_out = lax.all_to_all(copies, "seq", 0, 0, tiled=True)
    block_sum = own
    for part in (*near, far):
        block_sum += part.astype(jnp.float32)
    return (block_sum.astype(dtype), query_out)


def solution(mesh):
    return jax.shard_map(
        local,
        mesh=mesh,
        in_specs=(
            P("seq", "head"),
            P("seq", "head"),
            P("seq"),
            P(),
            P(None, "head"),
            P(None, "head"),
            P(None, "head"),
            P("head", None),
        ),
        out_specs=(P("seq", "head"), P(None, "head")),
        check_vma=False,
    )
```

```python
import jax
import jax.numpy as jnp
from jax import lax
from jax.experimental import pallas as pl
from jax.experimental.pallas import tpu as pltpu
from jax.sharding import PartitionSpec as P

HD = 128
LOG2_SCALE = HD ** (-0.5) * 1.4426950408889634
NEG = -1e30
PAIRS = 16
PLANE = [[2 * g + c for g in range(PAIRS)] for c in range(2)]
SWAP = [(i, i ^ 1) for i in range(2 * PAIRS)]
MIB = 1 << 20
VMEM = pl.BlockSpec(memory_space=pltpu.VMEM)
SMEM = pl.BlockSpec(memory_space=pltpu.SMEM)
ANY = pl.BlockSpec(memory_space=pl.ANY)
HBM = pl.BlockSpec(memory_space=pltpu.HBM)


def params(mib=52):
    return pltpu.CompilerParams(vmem_limit_bytes=mib * MIB)


def cost(flops, moved):
    return pl.CostEstimate(flops=flops, bytes_accessed=moved, transcendentals=0)


def plane_swap(blocks):
    return lax.all_to_all(blocks, "seq", 0, 0, axis_index_groups=PLANE, tiled=True)


def core_swap(block):
    return lax.ppermute(block, "seq", SWAP)


def head_shift(block, step):
    return lax.ppermute(block, "head", [(i, (i + step) % 4) for i in range(4)])


def exact_dot(a, b):
    return lax.dot_general(a, b, (((1,), (0,)), ((), ())), preferred_element_type=jnp.float32)


def score_dot(a, b):
    return lax.dot_general(a, b, (((1,), (1,)), ((), ())), preferred_element_type=jnp.float32)


def choose_kernel(counts, queries, tokens, out, held, sem):
    @pl.when(lax.axis_index("seq") == 0)
    def _():
        copy = pltpu.make_async_copy(tokens, held, sem)
        copy.start()
        copy.wait()
        row = lax.broadcasted_iota(jnp.int32, out.shape, 0)
        rows = held[...].astype(jnp.float32)
        out[...] = jnp.where(row < counts[0], rows, jnp.nan).astype(out.dtype)

    @pl.when(lax.axis_index("seq") != 0)
    def _():
        copy = pltpu.make_async_copy(queries, out, sem)
        copy.start()
        copy.wait()


def choose(counts, queries, tokens):
    return pl.pallas_call(
        choose_kernel,
        in_specs=[SMEM, ANY, ANY],
        out_specs=VMEM,
        out_shape=jax.ShapeDtypeStruct(tokens.shape, tokens.dtype),
        scratch_shapes=[pltpu.VMEM(tokens.shape, tokens.dtype), pltpu.SemaphoreType.DMA],
        compiler_params=params(4),
        cost_estimate=cost(1000, 2 * MIB),
    )(counts, queries, tokens)


def start_all(copies):
    for copy in copies:
        copy.start()
    return copies


def rows_of(step, size):
    return pl.ds(pl.multiple_of(((lax.axis_index("head") - step + 4) % 4) * size, size), size)


def few_kernel(fews, wq, wk, wv, pack_out, kv_out, held_q, held_kv, sems):
    size = fews.shape[2]
    nk = wk.shape[1]
    copies = []
    for step in range(4):
        rows = pl.ds(step * size, size)
        copies.append(
            start_all(
                [
                    pltpu.make_async_copy(wq.at[rows], held_q.at[step], sems.at[step, 0]),
                    pltpu.make_async_copy(wk.at[rows], held_kv.at[step, 0], sems.at[step, 1]),
                    pltpu.make_async_copy(wv.at[rows], held_kv.at[step, 1], sems.at[step, 2]),
                ]
            )
        )
    q = k = v = 0.0
    for step in range(4):
        for copy in copies[step]:
            copy.wait()
        few = fews[step]
        q += exact_dot(few, held_q[step])
        k += exact_dot(few, held_kv[step, 0])
        v += exact_dot(few, held_kv[step, 1])
    slab = fews.shape[1] // 2
    pack = jnp.concatenate([q[:slab], k[slab:], v[slab:]], axis=1)
    pack_out[...] = jnp.broadcast_to(pack[None], pack_out.shape).astype(pack_out.dtype)
    own = jnp.concatenate([k[:slab], v[:slab]], axis=1)
    kv_out[...] = jnp.concatenate([own, jnp.zeros_like(own)], axis=0).astype(kv_out.dtype)


def project_few(fews, w_query, w_key, w_value):
    depth = w_query.shape[0]
    few, size = fews.shape[1:]
    nq, nk = w_query.shape[1], w_key.shape[1]
    dtype = w_query.dtype
    return pl.pallas_call(
        few_kernel,
        in_specs=[VMEM] + [HBM] * 3,
        out_specs=[VMEM] * 2,
        out_shape=[
            jax.ShapeDtypeStruct((PAIRS, few // 2, nq + 2 * nk), dtype),
            jax.ShapeDtypeStruct((few, 2 * nk), dtype),
        ],
        scratch_shapes=[
            pltpu.VMEM((4, size, nq), dtype),
            pltpu.VMEM((4, 2, size, nk), dtype),
            pltpu.SemaphoreType.DMA((4, 3)),
        ],
        compiler_params=params(),
        cost_estimate=cost(2 * 128 * depth * (nq + 2 * nk), depth * (nq + 2 * nk) * 2),
    )(fews, w_query, w_key, w_value)


def chunk_copies(chunk, held, sems, at):
    half = chunk[0].shape[0]
    return [
        pltpu.make_async_copy(part, held.at[pl.ds(i * half, half)], sems.at[at + i])
        for i, part in enumerate(chunk)
    ]


def keys_kernel(*refs):
    (c0, c1, c2a, c2b, c3), (wk, wv, few, out, held, held_kv, acc, sems) = refs[:5], refs[5:]
    count, size = held.shape[1:]
    chunks = (c0,), (c1,), (c2a, c2b), (c3,)
    nk = wk.shape[1]
    copies = []
    for step in range(4):
        rows = rows_of(step, size)
        copies.append(
            start_all(
                [
                    pltpu.make_async_copy(wk.at[rows], held_kv.at[step, 0], sems.at[step, 0]),
                    pltpu.make_async_copy(wv.at[rows], held_kv.at[step, 1], sems.at[step, 1]),
                ]
                + chunk_copies(chunks[step], held.at[step], sems.at[step], 2)
            )
        )
    for step in range(4):
        for copy in copies[step]:
            copy.wait()
        for part in range(2):
            here = pl.ds(part * nk, nk)
            term = exact_dot(held[step], held_kv[step, part])
            if step == 0:
                acc[:, here] = term
            elif step < 3:
                acc[:, here] += term
            else:
                out[:count, here] = (acc[:, here] + term).astype(out.dtype)
    out[count:, :] = few[...]


def project_keys(chunks, w_key, w_value, few):
    rows, size = chunks[0].shape
    nk = w_key.shape[1]
    shape = (rows + few.shape[0], 2 * nk)
    dtype = w_key.dtype
    return pl.pallas_call(
        keys_kernel,
        in_specs=[ANY] * 5 + [HBM] * 2 + [VMEM],
        out_specs=VMEM,
        out_shape=jax.ShapeDtypeStruct(shape, dtype),
        scratch_shapes=[
            pltpu.VMEM((4, rows, size), dtype),
            pltpu.VMEM((4, 2, size, nk), dtype),
            pltpu.VMEM((rows, 2 * nk), jnp.float32),
            pltpu.SemaphoreType.DMA((4, 4)),
        ],
        compiler_params=params(),
        cost_estimate=cost(2 * rows * 4 * size * 2 * nk, 6 * MIB),
    )(*chunks, w_key, w_value, few)


def queries_kernel(*refs):
    (c0, c1, c2a, c2b, c3), (wq, out, held, held_q, acc, sems) = refs[:5], refs[5:]
    count, size = held.shape[1:]
    chunks = (c0,), (c1,), (c2a, c2b), (c3,)
    copies = []
    for step in range(4):
        rows = rows_of(step, size)
        copies.append(
            start_all(
                [
                    pltpu.make_async_copy(wq.at[rows], held_q.at[step], sems.at[step, 0]),
                ]
                + chunk_copies(chunks[step], held.at[step], sems.at[step], 1)
            )
        )
    for step in range(4):
        for copy in copies[step]:
            copy.wait()
        term = exact_dot(held[step], held_q[step])
        if step == 0:
            acc[...] = term
        elif step < 3:
            acc[...] += term
        else:
            out[...] = (acc[...] + term).astype(out.dtype)


def project_queries(chunks, w_query):
    rows, size = chunks[0].shape
    wide = w_query.shape[1]
    dtype = w_query.dtype
    return pl.pallas_call(
        queries_kernel,
        in_specs=[ANY] * 5 + [HBM],
        out_specs=VMEM,
        out_shape=jax.ShapeDtypeStruct((rows, wide), dtype),
        scratch_shapes=[
            pltpu.VMEM((4, rows, size), dtype),
            pltpu.VMEM((4, size, wide), dtype),
            pltpu.VMEM((rows, wide), jnp.float32),
            pltpu.SemaphoreType.DMA((4, 3)),
        ],
        compiler_params=params(),
        cost_estimate=cost(2 * rows * 4 * size * wide, 10 * MIB),
    )(*chunks, w_query)


def split(x):
    high = x.astype(jnp.bfloat16).astype(jnp.float32)
    middle = (x - high).astype(jnp.bfloat16).astype(jnp.float32)
    return [high, middle, x - high - middle]


def query_kernel(counts, sibling, q_ref, mine, other, out):
    seq = lax.axis_index("seq")
    core, pair, count_mine, count_other = seq % 2, seq // 2, counts[0], sibling[0]
    half = q_ref.shape[0]
    blk = 2 * half
    nk = mine.shape[1] // 2
    few = mine.shape[0] - blk
    slab = few // 2
    groups = nk // HD
    heads = (q_ref.shape[1] - 2 * nk) // HD
    local_row = lax.broadcasted_iota(jnp.int32, (HD, 2 * half), 1) % half
    row = local_row + slab * (local_row // slab + core)
    key = lax.broadcasted_iota(jnp.int32, (HD, 2 * half), 0)
    first = (2 * pair + core) * slab
    first_other = (2 * pair + 1 - core) * slab
    own_a = (key < slab) & (first + key <= row)
    own_b = (key >= few) & (key < few + slab) & (first_other + key - few <= row)
    block_key = lax.broadcasted_iota(jnp.int32, (blk, 2 * half), 0)
    seen = jnp.concatenate([block_key < count_mine, block_key < count_other, own_a | own_b], axis=0)
    fill = jnp.zeros((HD - 2 * few, HD), mine.dtype)
    tops, totals = [], []
    for g in range(groups):
        keys, values = (
            jnp.concatenate(
                [mine[:blk, c], other[:blk, c], mine[blk:, c], other[blk:, c], fill], axis=0
            )
            for c in (pl.ds(g * HD, HD), pl.ds(nk + g * HD, HD))
        )
        values = values.T
        for h in range(g * (heads // groups), (g + 1) * (heads // groups), 2):
            q = jnp.concatenate([q_ref[:, pl.ds((h + i) * HD, HD)] for i in range(2)], axis=0)
            s = jnp.where(seen, score_dot(keys, q), NEG)
            top = jnp.max(s, axis=0, keepdims=True)
            p = jnp.exp2((s - top) * LOG2_SCALE).astype(mine.dtype)
            total = jnp.sum(p.astype(jnp.float32), axis=0, keepdims=True)
            o = exact_dot(values, p).T.astype(out.dtype)
            for i in range(2):
                out[:, pl.ds((h + i) * HD, HD)] = o[i * half : (i + 1) * half]
                tops.append(top[:, i * half : (i + 1) * half])
                totals.append(total[:, i * half : (i + 1) * half])
    stats = [part for x in (tops, totals) for part in split(jnp.concatenate(x, axis=0))]
    pad = jnp.zeros((HD - 6 * heads, half), jnp.float32)
    out[:, pl.ds(heads * HD, HD)] = jnp.concatenate(stats + [pad], axis=0).T.astype(out.dtype)


def query_attention(counts, sibling, mine_rows, kv, kv_other):
    rows, wide = mine_rows.shape
    nq = wide - kv.shape[1]
    return pl.pallas_call(
        query_kernel,
        in_specs=[SMEM] * 2 + [VMEM] * 3,
        out_specs=VMEM,
        out_shape=jax.ShapeDtypeStruct((rows, nq + HD), kv.dtype),
        compiler_params=params(24),
        cost_estimate=cost(4 * rows * 640 * nq, 4 * MIB),
    )(counts, sibling, mine_rows, kv, kv_other)


ORDER = (2, 1, 3, 0)


def columns_of(step, size):
    return pl.ds(pl.multiple_of(((lax.axis_index("head") + step) % 4) * size, size), size)


def context_kernel(
    counts, q_ref, kv, a_mine, a_other, w_ref, out0, out1, out2, own, ctx, held, sems
):
    seq, count = lax.axis_index("seq"), counts[0]
    blk = q_ref.shape[0]
    width = own.shape[1]
    nk = kv.shape[1] // 2
    groups = nk // HD
    heads = q_ref.shape[1] // HD
    copies = [
        pltpu.make_async_copy(w_ref.at[:, columns_of(turn, width)], held.at[at], sems.at[at])
        for at, turn in enumerate(ORDER)
    ]
    start_all(copies)
    half = blk // 2
    key = lax.broadcasted_iota(jnp.int32, (blk, blk), 0)
    row = lax.broadcasted_iota(jnp.int32, (blk, blk), 1) % half
    own_seen = [(key <= row + at * half) & (key < count) for at in range(2)]
    front = jnp.zeros((blk, blk), jnp.int32) + seq > 0
    nq = q_ref.shape[1]
    for g in range(groups):
        kc, vc = pl.ds(g * HD, HD), pl.ds(nk + g * HD, HD)
        ac, bc = pl.ds(nq + g * HD, HD), pl.ds(nq + nk + g * HD, HD)
        ka = jnp.concatenate([a_mine[:, ac], a_other[:, kc]], axis=0)
        va = jnp.concatenate([a_mine[:, bc], a_other[:, vc]], axis=0)
        va = va.astype(jnp.float32)
        va = jnp.where(va == va, va, 0.0).astype(kv.dtype)
        keys = jnp.concatenate([ka, kv[:blk, kc]], axis=0)
        values = jnp.concatenate([va, kv[:blk, vc]], axis=0).T
        valid = None
        for h in range(g * (heads // groups), (g + 1) * (heads // groups), 2):
            for at in range(2):
                rows = pl.ds(at * half, half)
                size = blk + (at + 1) * half
                q = jnp.concatenate([q_ref[rows, pl.ds((h + i) * HD, HD)] for i in range(2)], axis=0)
                s = score_dot(keys[:size], q)
                if valid is None:
                    valid = front & (s[:blk] == s[:blk])
                seen = jnp.concatenate([valid, own_seen[at][: size - blk]], axis=0)
                s = jnp.where(seen, s, NEG)
                p = jnp.exp2((s - jnp.max(s, axis=0, keepdims=True)) * LOG2_SCALE)
                p = p * (1.0 / jnp.sum(p, axis=0, keepdims=True))
                o = exact_dot(values[:, :size], p.astype(kv.dtype)).T.astype(ctx.dtype)
                for i in range(2):
                    ctx[rows, pl.ds((h + i) * HD, HD)] = o[i * half : (i + 1) * half]
    for at in range(4):
        copies[at].wait()
        part = exact_dot(ctx[...], held[at])
        ref = (out0, out1, out2, own)[at]
        ref[...] = part.astype(ref.dtype)


def context(counts, q, kv, a_mine, a_other, w_out):
    blk, nq = q.shape
    depth, wide = w_out.shape
    width = wide // 4
    return pl.pallas_call(
        context_kernel,
        in_specs=[SMEM] + [VMEM] * 4 + [HBM],
        out_specs=[VMEM] * 4,
        out_shape=[jax.ShapeDtypeStruct((blk, width), q.dtype)] * 3
        + [jax.ShapeDtypeStruct((blk, width), jnp.float32)],
        scratch_shapes=[
            pltpu.VMEM((blk, nq), q.dtype),
            pltpu.VMEM((4, depth, width), q.dtype),
            pltpu.SemaphoreType.DMA((4,)),
        ],
        compiler_params=params(),
        cost_estimate=cost(4 * blk * 512 * nq + 2 * blk * depth * wide, 12 * MIB),
    )(counts, q, kv, a_mine, a_other, w_out)


def merge_kernel(parts, w_ref, out0, out1, out2, out3, held, sems):
    width = out0.shape[1]
    heads = (parts.shape[2] - HD) // HD
    copies = [
        pltpu.make_async_copy(w_ref.at[:, columns_of(at, width)], held.at[at], sems.at[at])
        for at in range(4)
    ]
    start_all(copies)
    stats = parts[:, :, pl.ds(heads * HD, HD)].astype(jnp.float32)
    stats = [stats[:, :, i * heads : (i + 1) * heads] for i in range(6)]
    m = stats[0] + stats[1] + stats[2]
    t = stats[3] + stats[4] + stats[5]
    scale = jnp.exp2((m - jnp.max(m, axis=0, keepdims=True)) * LOG2_SCALE)
    total = jnp.sum(scale * t, axis=0)
    ctx = []
    for h in range(heads):
        o = parts[:, :, pl.ds(h * HD, HD)].astype(jnp.float32)
        ctx.append(jnp.sum(scale[:, :, h : h + 1] * o, axis=0) / total[:, h : h + 1])
    ctx = jnp.concatenate(ctx, axis=1).astype(w_ref.dtype)
    for at in range(4):
        copies[at].wait()
        (out0, out1, out2, out3)[at][...] = exact_dot(ctx, held[at])


def merge(parts, w_out):
    slab = parts.shape[1]
    depth, wide = w_out.shape
    width = wide // 4
    return pl.pallas_call(
        merge_kernel,
        in_specs=[VMEM, HBM],
        out_specs=[VMEM] * 4,
        out_shape=[jax.ShapeDtypeStruct((slab, width), jnp.float32)] * 4,
        scratch_shapes=[
            pltpu.VMEM((4, depth, width), w_out.dtype),
            pltpu.SemaphoreType.DMA((4,)),
        ],
        compiler_params=params(),
        cost_estimate=cost(2 * 128 * depth * wide, depth * wide * 2),
    )(parts, w_out)


def total_kernel(a, b, c, d, out):
    total = (a[...] + b[...]) + (c[...] + d[...])
    total = jnp.concatenate([total, total], axis=0).astype(out.dtype)
    for at in range(0, out.shape[0], total.shape[0]):
        out[pl.ds(at, total.shape[0]), :] = total


def local(tokens, queries, valid_counts, query_host, w_query, w_key, w_value, w_out):
    host = query_host[0]
    blk, width = tokens.shape
    slab = blk // (2 * PAIRS)
    dtype = tokens.dtype
    half = blk // 2
    right, left = head_shift(tokens, 1), head_shift(tokens, 3)
    sibling = core_swap(valid_counts)

    sent = lax.cond(
        host == 0,
        lambda q, t: choose(valid_counts, core_swap(q), t),
        lambda q, t: choose(valid_counts, q, t),
        queries,
        tokens,
    )
    source = (jnp.maximum(host, 1) * slab).astype(jnp.uint32)
    sent, source = lax.optimization_barrier((sent, source))
    spread = lax.all_to_all(sent, "seq", 0, 0, tiled=True)
    zero = jnp.zeros_like(source)
    picked = jnp.concatenate(
        [lax.dynamic_slice(spread, (source, zero), (slab, width)), spread[:slab]], axis=0
    )
    picked, sibling = lax.optimization_barrier((picked, sibling))
    copies = jnp.broadcast_to(picked[None], (4,) + picked.shape)
    fews = lax.all_to_all(copies, "head", 0, 0, tiled=True)
    right_half, left_half, _ = lax.optimization_barrier((right[:half], left[half:], picked))
    chunks = [tokens, right, head_shift(right_half, 1), head_shift(left_half, 3), left]
    pack, few_kv = project_few(fews, w_query, w_key, w_value)
    mine = plane_swap(pack).reshape(blk // 2, -1)
    kv = project_keys(chunks, w_key, w_value, few_kv)
    kv_other = core_swap(kv)
    chunks[0], kv = lax.optimization_barrier((chunks[0], kv))
    q_blk = project_queries(chunks, w_query)
    mine, q_blk = lax.optimization_barrier((mine, q_blk))
    mine_other = core_swap(mine[:, w_query.shape[1] :])

    stats = query_attention(valid_counts, sibling, mine, kv, kv_other)
    merged = plane_swap(stats.reshape(PAIRS, slab, -1))
    far, after, before, own = context(valid_counts, q_blk, kv, mine, mine_other, w_out)
    merged, own, before, far = lax.optimization_barrier((merged, own, before, far))
    term = merge(merged, w_out)
    parts = [term[0]] + [head_shift(term[step], step) for step in (1, 2, 3)]
    before, _ = lax.optimization_barrier((before, term[0]))
    near = head_shift(after, 1), head_shift(before, 3)
    copies = pl.pallas_call(
        total_kernel,
        out_shape=jax.ShapeDtypeStruct((blk, width), dtype),
        compiler_params=params(24),
    )(*parts)
    far, copies = lax.optimization_barrier((far, copies))
    far = head_shift(far, 2)
    query_out = lax.all_to_all(copies, "seq", 0, 0, tiled=True)
    block_sum = own
    for part in (*near, far):
        block_sum += part.astype(jnp.float32)
    return (block_sum.astype(dtype), query_out)


def solution(mesh):
    return jax.shard_map(
        local,
        mesh=mesh,
        in_specs=(
            P("seq", "head"),
            P("seq", "head"),
            P("seq"),
            P(),
            P(None, "head"),
            P(None, "head"),
            P(None, "head"),
            P("head", None),
        ),
        out_specs=(P("seq", "head"), P(None, "head")),
        check_vma=False,
    )
```

```python
import jax
import jax.numpy as jnp
from jax import lax
from jax.experimental import pallas as pl
from jax.experimental.pallas import tpu as pltpu
from jax.sharding import PartitionSpec as P

HD = 128
LOG2_SCALE = HD ** (-0.5) * 1.4426950408889634
NEG = -1e30
PAIRS = 16
PLANE = [[2 * g + c for g in range(PAIRS)] for c in range(2)]
SWAP = [(i, i ^ 1) for i in range(2 * PAIRS)]
MIB = 1 << 20
VMEM = pl.BlockSpec(memory_space=pltpu.VMEM)
SMEM = pl.BlockSpec(memory_space=pltpu.SMEM)
ANY = pl.BlockSpec(memory_space=pl.ANY)
HBM = pl.BlockSpec(memory_space=pltpu.HBM)


def params(mib=52):
    return pltpu.CompilerParams(vmem_limit_bytes=mib * MIB)


def cost(flops, moved):
    return pl.CostEstimate(flops=flops, bytes_accessed=moved, transcendentals=0)


def plane_swap(blocks):
    return lax.all_to_all(blocks, "seq", 0, 0, axis_index_groups=PLANE, tiled=True)


def core_swap(block):
    return lax.ppermute(block, "seq", SWAP)


def head_shift(block, step):
    return lax.ppermute(block, "head", [(i, (i + step) % 4) for i in range(4)])


def exact_dot(a, b):
    return lax.dot_general(a, b, (((1,), (0,)), ((), ())), preferred_element_type=jnp.float32)


def score_dot(a, b):
    return lax.dot_general(a, b, (((1,), (1,)), ((), ())), preferred_element_type=jnp.float32)


def choose_kernel(counts, queries, tokens, out, held, sem):
    @pl.when(lax.axis_index("seq") == 0)
    def _():
        copy = pltpu.make_async_copy(tokens, held, sem)
        copy.start()
        copy.wait()
        row = lax.broadcasted_iota(jnp.int32, out.shape, 0)
        rows = held[...].astype(jnp.float32)
        out[...] = jnp.where(row < counts[0], rows, jnp.nan).astype(out.dtype)

    @pl.when(lax.axis_index("seq") != 0)
    def _():
        copy = pltpu.make_async_copy(queries, out, sem)
        copy.start()
        copy.wait()


def choose(counts, queries, tokens):
    return pl.pallas_call(
        choose_kernel,
        in_specs=[SMEM, ANY, ANY],
        out_specs=VMEM,
        out_shape=jax.ShapeDtypeStruct(tokens.shape, tokens.dtype),
        scratch_shapes=[pltpu.VMEM(tokens.shape, tokens.dtype), pltpu.SemaphoreType.DMA],
        compiler_params=params(4),
        cost_estimate=cost(1000, 2 * MIB),
    )(counts, queries, tokens)


def start_all(copies):
    for copy in copies:
        copy.start()
    return copies


def rows_of(step, size):
    return pl.ds(pl.multiple_of(((lax.axis_index("head") - step + 4) % 4) * size, size), size)


def few_kernel(fews, wq, wk, wv, pack_out, kv_out, held_q, held_kv, sems):
    size = fews.shape[2]
    nk = wk.shape[1]
    copies = []
    for step in range(4):
        rows = pl.ds(step * size, size)
        copies.append(
            start_all(
                [
                    pltpu.make_async_copy(wq.at[rows], held_q.at[step], sems.at[step, 0]),
                    pltpu.make_async_copy(wk.at[rows], held_kv.at[step, 0], sems.at[step, 1]),
                    pltpu.make_async_copy(wv.at[rows], held_kv.at[step, 1], sems.at[step, 2]),
                ]
            )
        )
    q = k = v = 0.0
    for step in range(4):
        for copy in copies[step]:
            copy.wait()
        few = fews[step]
        q += exact_dot(few, held_q[step])
        k += exact_dot(few, held_kv[step, 0])
        v += exact_dot(few, held_kv[step, 1])
    slab = fews.shape[1] // 2
    pack = jnp.concatenate([q[:slab], k[slab:], v[slab:]], axis=1)
    pack_out[...] = jnp.broadcast_to(pack[None], pack_out.shape).astype(pack_out.dtype)
    own = jnp.concatenate([k[:slab], v[:slab]], axis=1)
    kv_out[...] = jnp.concatenate([own, jnp.zeros_like(own)], axis=0).astype(kv_out.dtype)


def project_few(fews, w_query, w_key, w_value):
    depth = w_query.shape[0]
    few, size = fews.shape[1:]
    nq, nk = w_query.shape[1], w_key.shape[1]
    dtype = w_query.dtype
    return pl.pallas_call(
        few_kernel,
        in_specs=[VMEM] + [HBM] * 3,
        out_specs=[VMEM] * 2,
        out_shape=[
            jax.ShapeDtypeStruct((PAIRS, few // 2, nq + 2 * nk), dtype),
            jax.ShapeDtypeStruct((few, 2 * nk), dtype),
        ],
        scratch_shapes=[
            pltpu.VMEM((4, size, nq), dtype),
            pltpu.VMEM((4, 2, size, nk), dtype),
            pltpu.SemaphoreType.DMA((4, 3)),
        ],
        compiler_params=params(),
        cost_estimate=cost(2 * 128 * depth * (nq + 2 * nk), depth * (nq + 2 * nk) * 2),
    )(fews, w_query, w_key, w_value)


def chunk_copies(chunk, held, sems, at):
    half = chunk[0].shape[0]
    return [
        pltpu.make_async_copy(part, held.at[pl.ds(i * half, half)], sems.at[at + i])
        for i, part in enumerate(chunk)
    ]


def keys_kernel(*refs):
    (c0, c1, c2a, c2b, c3), (wk, wv, few, out, held, held_kv, acc, sems) = refs[:5], refs[5:]
    count, size = held.shape[1:]
    chunks = (c0,), (c1,), (c2a, c2b), (c3,)
    nk = wk.shape[1]
    copies = []
    for step in range(4):
        rows = rows_of(step, size)
        copies.append(
            start_all(
                [
                    pltpu.make_async_copy(wk.at[rows], held_kv.at[step, 0], sems.at[step, 0]),
                    pltpu.make_async_copy(wv.at[rows], held_kv.at[step, 1], sems.at[step, 1]),
                ]
                + chunk_copies(chunks[step], held.at[step], sems.at[step], 2)
            )
        )
    for step in range(4):
        for copy in copies[step]:
            copy.wait()
        for part in range(2):
            here = pl.ds(part * nk, nk)
            term = exact_dot(held[step], held_kv[step, part])
            if step == 0:
                acc[:, here] = term
            elif step < 3:
                acc[:, here] += term
            else:
                out[:count, here] = (acc[:, here] + term).astype(out.dtype)
    out[count:, :] = few[...]


def project_keys(chunks, w_key, w_value, few):
    rows, size = chunks[0].shape
    nk = w_key.shape[1]
    shape = (rows + few.shape[0], 2 * nk)
    dtype = w_key.dtype
    return pl.pallas_call(
        keys_kernel,
        in_specs=[ANY] * 5 + [HBM] * 2 + [VMEM],
        out_specs=VMEM,
        out_shape=jax.ShapeDtypeStruct(shape, dtype),
        scratch_shapes=[
            pltpu.VMEM((4, rows, size), dtype),
            pltpu.VMEM((4, 2, size, nk), dtype),
            pltpu.VMEM((rows, 2 * nk), jnp.float32),
            pltpu.SemaphoreType.DMA((4, 4)),
        ],
        compiler_params=params(),
        cost_estimate=cost(2 * rows * 4 * size * 2 * nk, 6 * MIB),
    )(*chunks, w_key, w_value, few)


def queries_kernel(*refs):
    (c0, c1, c2a, c2b, c3), (wq, out, held, held_q, acc, sems) = refs[:5], refs[5:]
    count, size = held.shape[1:]
    chunks = (c0,), (c1,), (c2a, c2b), (c3,)
    copies = []
    for step in range(4):
        rows = rows_of(step, size)
        copies.append(
            start_all(
                [
                    pltpu.make_async_copy(wq.at[rows], held_q.at[step], sems.at[step, 0]),
                ]
                + chunk_copies(chunks[step], held.at[step], sems.at[step], 1)
            )
        )
    for step in range(4):
        for copy in copies[step]:
            copy.wait()
        term = exact_dot(held[step], held_q[step])
        if step == 0:
            acc[...] = term
        elif step < 3:
            acc[...] += term
        else:
            out[...] = (acc[...] + term).astype(out.dtype)


def project_queries(chunks, w_query):
    rows, size = chunks[0].shape
    wide = w_query.shape[1]
    dtype = w_query.dtype
    return pl.pallas_call(
        queries_kernel,
        in_specs=[ANY] * 5 + [HBM],
        out_specs=VMEM,
        out_shape=jax.ShapeDtypeStruct((rows, wide), dtype),
        scratch_shapes=[
            pltpu.VMEM((4, rows, size), dtype),
            pltpu.VMEM((4, size, wide), dtype),
            pltpu.VMEM((rows, wide), jnp.float32),
            pltpu.SemaphoreType.DMA((4, 3)),
        ],
        compiler_params=params(),
        cost_estimate=cost(2 * rows * 4 * size * wide, 10 * MIB),
    )(*chunks, w_query)


def split(x):
    high = x.astype(jnp.bfloat16).astype(jnp.float32)
    middle = (x - high).astype(jnp.bfloat16).astype(jnp.float32)
    return [high, middle, x - high - middle]


def query_kernel(counts, sibling, q_ref, mine, other, out):
    seq = lax.axis_index("seq")
    core, pair, count_mine, count_other = seq % 2, seq // 2, counts[0], sibling[0]
    half = q_ref.shape[0]
    blk = 2 * half
    nk = mine.shape[1] // 2
    few = mine.shape[0] - blk
    slab = few // 2
    groups = nk // HD
    heads = (q_ref.shape[1] - 2 * nk) // HD
    local_row = lax.broadcasted_iota(jnp.int32, (HD, 2 * half), 1) % half
    row = local_row + slab * (local_row // slab + core)
    key = lax.broadcasted_iota(jnp.int32, (HD, 2 * half), 0)
    first = (2 * pair + core) * slab
    first_other = (2 * pair + 1 - core) * slab
    own_a = (key < slab) & (first + key <= row)
    own_b = (key >= few) & (key < few + slab) & (first_other + key - few <= row)
    block_key = lax.broadcasted_iota(jnp.int32, (blk, 2 * half), 0)
    seen = jnp.concatenate([block_key < count_mine, block_key < count_other, own_a | own_b], axis=0)
    fill = jnp.zeros((HD - 2 * few, HD), mine.dtype)
    tops, totals = [], []
    for g in range(groups):
        keys, values = (
            jnp.concatenate(
                [mine[:blk, c], other[:blk, c], mine[blk:, c], other[blk:, c], fill], axis=0
            )
            for c in (pl.ds(g * HD, HD), pl.ds(nk + g * HD, HD))
        )
        values = values.T
        for h in range(g * (heads // groups), (g + 1) * (heads // groups), 2):
            q = jnp.concatenate([q_ref[:, pl.ds((h + i) * HD, HD)] for i in range(2)], axis=0)
            s = jnp.where(seen, score_dot(keys, q), NEG)
            top = jnp.max(s, axis=0, keepdims=True)
            p = jnp.exp2((s - top) * LOG2_SCALE).astype(mine.dtype)
            total = jnp.sum(p.astype(jnp.float32), axis=0, keepdims=True)
            o = exact_dot(values, p).T.astype(out.dtype)
            for i in range(2):
                out[:, pl.ds((h + i) * HD, HD)] = o[i * half : (i + 1) * half]
                tops.append(top[:, i * half : (i + 1) * half])
                totals.append(total[:, i * half : (i + 1) * half])
    stats = [part for x in (tops, totals) for part in split(jnp.concatenate(x, axis=0))]
    pad = jnp.zeros((HD - 6 * heads, half), jnp.float32)
    out[:, pl.ds(heads * HD, HD)] = jnp.concatenate(stats + [pad], axis=0).T.astype(out.dtype)


def query_attention(counts, sibling, mine_rows, kv, kv_other):
    rows, wide = mine_rows.shape
    nq = wide - kv.shape[1]
    return pl.pallas_call(
        query_kernel,
        in_specs=[SMEM] * 2 + [VMEM] * 3,
        out_specs=VMEM,
        out_shape=jax.ShapeDtypeStruct((rows, nq + HD), kv.dtype),
        compiler_params=params(24),
        cost_estimate=cost(4 * rows * 640 * nq, 4 * MIB),
    )(counts, sibling, mine_rows, kv, kv_other)


ORDER = (2, 1, 3, 0)


def columns_of(step, size):
    return pl.ds(pl.multiple_of(((lax.axis_index("head") + step) % 4) * size, size), size)


def context_kernel(
    counts, q_ref, kv, a_mine, a_other, w_ref, out0, out1, out2, own, ctx, held, sems
):
    seq, count = lax.axis_index("seq"), counts[0]
    blk = q_ref.shape[0]
    width = own.shape[1]
    nk = kv.shape[1] // 2
    groups = nk // HD
    heads = q_ref.shape[1] // HD
    copies = [
        pltpu.make_async_copy(w_ref.at[:, columns_of(turn, width)], held.at[at], sems.at[at])
        for at, turn in enumerate(ORDER)
    ]
    start_all(copies)
    half = blk // 2
    key = lax.broadcasted_iota(jnp.int32, (blk, blk), 0)
    row = lax.broadcasted_iota(jnp.int32, (blk, blk), 1) % half
    own_seen = [(key <= row + at * half) & (key < count) for at in range(2)]
    front = jnp.zeros((blk, blk), jnp.int32) + seq > 0
    nq = q_ref.shape[1]
    for g in range(groups):
        kc, vc = pl.ds(g * HD, HD), pl.ds(nk + g * HD, HD)
        ac, bc = pl.ds(nq + g * HD, HD), pl.ds(nq + nk + g * HD, HD)
        ka = jnp.concatenate([a_mine[:, ac], a_other[:, kc]], axis=0)
        va = jnp.concatenate([a_mine[:, bc], a_other[:, vc]], axis=0)
        va = va.astype(jnp.float32)
        va = jnp.where(va == va, va, 0.0).astype(kv.dtype)
        keys = jnp.concatenate([ka, kv[:blk, kc]], axis=0)
        values = jnp.concatenate([va, kv[:blk, vc]], axis=0).T
        valid = None
        for h in range(g * (heads // groups), (g + 1) * (heads // groups), 2):
            for at in range(2):
                rows = pl.ds(at * half, half)
                size = blk + (at + 1) * half
                q = jnp.concatenate([q_ref[rows, pl.ds((h + i) * HD, HD)] for i in range(2)], axis=0)
                s = score_dot(keys[:size], q)
                if valid is None:
                    valid = front & (s[:blk] == s[:blk])
                seen = jnp.concatenate([valid, own_seen[at][: size - blk]], axis=0)
                s = jnp.where(seen, s, NEG)
                p = jnp.exp2((s - jnp.max(s, axis=0, keepdims=True)) * LOG2_SCALE)
                p = p * (1.0 / jnp.sum(p, axis=0, keepdims=True))
                o = exact_dot(values[:, :size], p.astype(kv.dtype)).T.astype(ctx.dtype)
                for i in range(2):
                    ctx[rows, pl.ds((h + i) * HD, HD)] = o[i * half : (i + 1) * half]
    for at in range(4):
        copies[at].wait()
        part = exact_dot(ctx[...], held[at])
        ref = (out0, out1, out2, own)[at]
        ref[...] = part.astype(ref.dtype)


def context(counts, q, kv, a_mine, a_other, w_out):
    blk, nq = q.shape
    depth, wide = w_out.shape
    width = wide // 4
    return pl.pallas_call(
        context_kernel,
        in_specs=[SMEM] + [VMEM] * 4 + [HBM],
        out_specs=[VMEM] * 4,
        out_shape=[jax.ShapeDtypeStruct((blk, width), q.dtype)] * 3
        + [jax.ShapeDtypeStruct((blk, width), jnp.float32)],
        scratch_shapes=[
            pltpu.VMEM((blk, nq), q.dtype),
            pltpu.VMEM((4, depth, width), q.dtype),
            pltpu.SemaphoreType.DMA((4,)),
        ],
        compiler_params=params(),
        cost_estimate=cost(4 * blk * 512 * nq + 2 * blk * depth * wide, 12 * MIB),
    )(counts, q, kv, a_mine, a_other, w_out)


def merge_kernel(parts, w_ref, out0, out1, out2, out3, held, sems):
    width = out0.shape[1]
    heads = (parts.shape[2] - HD) // HD
    copies = [
        pltpu.make_async_copy(w_ref.at[:, columns_of(at, width)], held.at[at], sems.at[at])
        for at in range(4)
    ]
    start_all(copies)
    stats = parts[:, :, pl.ds(heads * HD, HD)].astype(jnp.float32)
    stats = [stats[:, :, i * heads : (i + 1) * heads] for i in range(6)]
    m = stats[0] + stats[1] + stats[2]
    t = stats[3] + stats[4] + stats[5]
    scale = jnp.exp2((m - jnp.max(m, axis=0, keepdims=True)) * LOG2_SCALE)
    total = jnp.sum(scale * t, axis=0)
    ctx = []
    for h in range(heads):
        o = parts[:, :, pl.ds(h * HD, HD)].astype(jnp.float32)
        ctx.append(jnp.sum(scale[:, :, h : h + 1] * o, axis=0) / total[:, h : h + 1])
    ctx = jnp.concatenate(ctx, axis=1).astype(w_ref.dtype)
    for at in range(4):
        copies[at].wait()
        (out0, out1, out2, out3)[at][...] = exact_dot(ctx, held[at])


def merge(parts, w_out):
    slab = parts.shape[1]
    depth, wide = w_out.shape
    width = wide // 4
    return pl.pallas_call(
        merge_kernel,
        in_specs=[VMEM, HBM],
        out_specs=[VMEM] * 4,
        out_shape=[jax.ShapeDtypeStruct((slab, width), jnp.float32)] * 4,
        scratch_shapes=[
            pltpu.VMEM((4, depth, width), w_out.dtype),
            pltpu.SemaphoreType.DMA((4,)),
        ],
        compiler_params=params(),
        cost_estimate=cost(2 * 128 * depth * wide, depth * wide * 2),
    )(parts, w_out)


def total_kernel(a, b, c, d, out):
    total = (a[...] + b[...]) + (c[...] + d[...])
    total = jnp.concatenate([total, total], axis=0).astype(out.dtype)
    for at in range(0, out.shape[0], total.shape[0]):
        out[pl.ds(at, total.shape[0]), :] = total


def finish_kernel(own, a, b, c, query, block_out, query_out, staged, sems):
    query_copy = pltpu.make_async_copy(query, query_out, sems.at[0])
    query_copy.start()
    total = own[...] + a[...].astype(jnp.float32)
    total = total + b[...].astype(jnp.float32) + c[...].astype(jnp.float32)
    staged[...] = total.astype(staged.dtype)
    block_copy = pltpu.make_async_copy(staged, block_out, sems.at[1])
    block_copy.start()
    query_copy.wait()
    block_copy.wait()


def finish(*refs):
    query = refs[-1]
    return pl.pallas_call(
        finish_kernel,
        in_specs=[VMEM] * 5,
        out_specs=[ANY] * 2,
        out_shape=[jax.ShapeDtypeStruct(query.shape, query.dtype)] * 2,
        scratch_shapes=[
            pltpu.VMEM(query.shape, query.dtype),
            pltpu.SemaphoreType.DMA((2,)),
        ],
        compiler_params=params(24),
        cost_estimate=cost(1000, 4 * MIB),
    )(*refs)


def local(tokens, queries, valid_counts, query_host, w_query, w_key, w_value, w_out):
    host = query_host[0]
    blk, width = tokens.shape
    slab = blk // (2 * PAIRS)
    dtype = tokens.dtype
    half = blk // 2
    right, left = head_shift(tokens, 1), head_shift(tokens, 3)
    sibling = core_swap(valid_counts)

    sent = lax.cond(
        host == 0,
        lambda q, t: choose(valid_counts, core_swap(q), t),
        lambda q, t: choose(valid_counts, q, t),
        queries,
        tokens,
    )
    source = (jnp.maximum(host, 1) * slab).astype(jnp.uint32)
    sent, source = lax.optimization_barrier((sent, source))
    spread = lax.all_to_all(sent, "seq", 0, 0, tiled=True)
    zero = jnp.zeros_like(source)
    picked = jnp.concatenate(
        [lax.dynamic_slice(spread, (source, zero), (slab, width)), spread[:slab]], axis=0
    )
    picked, sibling = lax.optimization_barrier((picked, sibling))
    copies = jnp.broadcast_to(picked[None], (4,) + picked.shape)
    fews = lax.all_to_all(copies, "head", 0, 0, tiled=True)
    right_half, left_half, _ = lax.optimization_barrier((right[:half], left[half:], picked))
    chunks = [tokens, right, head_shift(right_half, 1), head_shift(left_half, 3), left]
    pack, few_kv = project_few(fews, w_query, w_key, w_value)
    mine = plane_swap(pack).reshape(blk // 2, -1)
    kv = project_keys(chunks, w_key, w_value, few_kv)
    kv_other = core_swap(kv)
    chunks[0], kv = lax.optimization_barrier((chunks[0], kv))
    q_blk = project_queries(chunks, w_query)
    mine, q_blk = lax.optimization_barrier((mine, q_blk))
    mine_other = core_swap(mine[:, w_query.shape[1] :])

    stats = query_attention(valid_counts, sibling, mine, kv, kv_other)
    merged = plane_swap(stats.reshape(PAIRS, slab, -1))
    far, after, before, own = context(valid_counts, q_blk, kv, mine, mine_other, w_out)
    merged, own, before, far = lax.optimization_barrier((merged, own, before, far))
    term = merge(merged, w_out)
    parts = [term[0]] + [head_shift(term[step], step) for step in (1, 2, 3)]
    before, _ = lax.optimization_barrier((before, term[0]))
    near = head_shift(after, 1), head_shift(before, 3)
    copies = pl.pallas_call(
        total_kernel,
        out_shape=jax.ShapeDtypeStruct((blk, width), dtype),
        compiler_params=params(24),
    )(*parts)
    far, copies = lax.optimization_barrier((far, copies))
    far = head_shift(far, 2)
    query_out = lax.all_to_all(copies, "seq", 0, 0, tiled=True)
    return tuple(finish(own, *near, far, query_out))


def solution(mesh):
    return jax.shard_map(
        local,
        mesh=mesh,
        in_specs=(
            P("seq", "head"),
            P("seq", "head"),
            P("seq"),
            P(),
            P(None, "head"),
            P(None, "head"),
            P(None, "head"),
            P("head", None),
        ),
        out_specs=(P("seq", "head"), P(None, "head")),
        check_vma=False,
    )
```
